128 devices in a mesh: leaf: 8 (over z, core), row: 16 (over x, y).
Axes of the slice: x: 4, y: 4, z: 4, core: 2. Of those that a mesh axis runs over, the one named last changes fastest.
Arguments:
- points: float32 [65536, 64], P(('leaf', 'row')), may hold values from -6 to 6
- samples: float32 [65536, 512], P(('leaf', 'row')), may hold values from -6 to 6
- test_matrix: float32 [65536, 512], P(('leaf', 'row')), may hold values from -0.0625 to 0.0625
- near_mask: int32 [8, 2], P('leaf'), may hold values from 0 to 1, as said below
- leaf_pivots: int32 [8, 256], P('leaf'), may hold values from 0 to 8191, as said below
- mid_pivots: int32 [4, 256], replicated, may hold values from 0 to 511, as said below
- top_pivots: int32 [2, 256], replicated, may hold values from 0 to 511, as said below
Outputs:
- leaf_basis: float32 [65536, 256], P(('leaf', 'row'))
- mid_basis: float32 [2048, 256], P(('leaf', 'row'))
- top_basis: float32 [1024, 256], P(('leaf', 'row'))
The draws below stay inside these ranges and needn't reach their ends.
Inputs may be any that keep to these rules, and one draw needn't show every extreme that they name: Siblings are always near: near_mask[c, 1] is 1 for even c and near_mask[c, 0] is 1 for odd c; the other entry of each row is 0 or 1. `leaf_pivots`: each row holds 256 distinct values, among them 0 and 8191. `mid_pivots`: each row holds 256 distinct values, among them 0 and 511. `top_pivots`: each row holds 256 distinct values, among them 0 and 511.
All inputs are finite; a program needn't handle non-finite values.
Results may differ from the reference program's by a relative error of at most 0.0003.
Values sent between devices are 32-bit elements; how exact they have to be, the bound alone decides.
No kernel may reach another device: no remote copies, remote signals or barrier semaphores. Data moves between devices by JAX's collectives and lax.ppermute only.
A program may use at most 256 MiB of HBM per device.

```python
import jax
import jax.numpy as jnp
from jax import lax

DIM = 64
RANK = 256
SAMP = 512
LEAVES = 8
MIDS = 4
TOPS = 2
CLUSTER = 8192
NPTS = 65536


def pivot_rows(key, row_count, span):
    keys = jax.random.split(key, row_count)

    def single(row_key):
        inner_vals = jax.random.permutation(row_key, span - 2)[:RANK - 2].astype(jnp.int32) + 1
        ends = jnp.array([0, span - 1], dtype=jnp.int32)
        joined = jnp.concatenate([ends, inner_vals])
        return jax.random.permutation(jax.random.fold_in(row_key, 7), joined).astype(jnp.int32)
    return jax.vmap(single)(keys)


def draw_near_mask(key, part):
    key = jax.random.fold_in(key, 5)
    random_flags = jax.random.randint(key, (LEAVES, 2), 0, 2).astype(jnp.int32)
    parity = jnp.arange(LEAVES, dtype=jnp.int32) % 2
    before_flag = jnp.where(parity == 1, 1, random_flags[:, 0]).astype(jnp.int32)
    after_flag = jnp.where(parity == 0, 1, random_flags[:, 1]).astype(jnp.int32)
    return jnp.stack([before_flag, after_flag], axis=1).astype(jnp.int32)


def draw_leaf_pivots(key, part):
    return pivot_rows(jax.random.fold_in(key, 11), LEAVES, CLUSTER)


def draw_mid_pivots(key, part):
    return pivot_rows(jax.random.fold_in(key, 23), MIDS, 2 * RANK)


def draw_top_pivots(key, part):
    return pivot_rows(jax.random.fold_in(key, 37), TOPS, 2 * RANK)


def block_levels(stream_key, dims, cuts, smallest, largest):
    gain = 1.0
    for position, parts in cuts:
        steps = jax.random.uniform(jax.random.fold_in(jax.random.fold_in(stream_key, 6), position), (parts,), jnp.float32, smallest / len(cuts), largest / len(cuts))
        gain = gain * jnp.repeat(jnp.exp(steps), dims[position] // parts).reshape((-1,) + (1,) * (len(dims) - 1 - position))
    return gain


def normal_values(rng, dims, deviation, bound, shards=(), kind=jnp.bfloat16):
    drawn = jax.random.normal(rng, dims, jnp.float32) * deviation
    if len(shards) > 0:
        drawn = block_levels(rng, dims, shards, -0.22, 0.18) * drawn
    return jnp.clip(drawn, min=-bound, max=bound).astype(kind)


def setup_inputs(seed: int = 0) -> dict:
    streams_of = jax.random.split(jax.random.key(seed), 8)
    return {
        "points": normal_values(streams_of[0], (NPTS, DIM), 1.0, 6.0, ((0, 128),), jnp.float32),
        "samples": normal_values(streams_of[1], (NPTS, SAMP), 1.0, 6.0, ((0, 128),), jnp.float32),
        "test_matrix": normal_values(streams_of[2], (NPTS, SAMP), CLUSTER ** -0.5, 0.0625, ((0, 128),), jnp.float32),
        "near_mask": draw_near_mask(jax.random.fold_in(streams_of[7], 71), 0),
        "leaf_pivots": draw_leaf_pivots(jax.random.fold_in(streams_of[7], 71), 0),
        "mid_pivots": draw_mid_pivots(jax.random.fold_in(streams_of[7], 71), 0),
        "top_pivots": draw_top_pivots(jax.random.fold_in(streams_of[7], 71), 0),
    }


HIGHEST = lax.Precision.HIGHEST

def kernel(source, target):
    source_sq = jnp.sum(source * source, axis=1)
    target_sq = jnp.sum(target * target, axis=1)
    inner_prod = jnp.dot(source, target.T, precision=HIGHEST)
    return jnp.exp(-(source_sq[:, None] + target_sq[None, :] - 2.0 * inner_prod) / DIM)

def contract_rows(first_mat, second_mat):
    return lax.dot_general(first_mat, second_mat, (((0,), (0,)), ((), ())), precision=HIGHEST)

def solve_coeffs(picked):
    gram_matrix = jnp.dot(picked, picked.T, precision=HIGHEST)
    ridge_shift = jnp.trace(gram_matrix) / RANK + 1e-06
    gram_matrix = gram_matrix + ridge_shift * jnp.eye(RANK, dtype=jnp.float32)
    factor = jnp.linalg.cholesky(gram_matrix)
    return jax.scipy.linalg.cho_solve((factor, True), picked)

def combine(first_node, second_node, pivots):
    coupling = kernel(first_node[0], second_node[0])
    upper_half = first_node[1] - jnp.dot(coupling, second_node[2], precision=HIGHEST)
    lower_half = second_node[1] - contract_rows(coupling, first_node[2])
    stacked = jnp.concatenate([upper_half, lower_half], axis=0)
    skel_stack = jnp.concatenate([first_node[0], second_node[0]], axis=0)
    proj_stack = jnp.concatenate([first_node[2], second_node[2]], axis=0)
    picked = jnp.take(stacked, pivots, axis=0)
    coeffs = solve_coeffs(picked)
    basis_rows = jnp.dot(stacked, coeffs.T, precision=HIGHEST)
    projection = jnp.dot(coeffs, contract_rows(stacked, proj_stack), precision=HIGHEST)
    return (basis_rows, (jnp.take(skel_stack, pivots, axis=0), picked, projection))

def reference(points, samples, test_matrix, near_mask, leaf_pivots, mid_pivots, top_pivots):
    cluster_pts = points.reshape(LEAVES, CLUSTER, DIM)
    cluster_samp = samples.reshape(LEAVES, CLUSTER, SAMP)
    cluster_test = test_matrix.reshape(LEAVES, CLUSTER, SAMP)

    def leaf_node(node_index):
        own_pts = cluster_pts[node_index]
        before = jnp.maximum(node_index - 1, 0)
        following = jnp.minimum(node_index + 1, LEAVES - 1)
        weight_before = near_mask[node_index, 0].astype(jnp.float32) * (node_index > 0).astype(jnp.float32)
        weight_after = near_mask[node_index, 1].astype(jnp.float32) * (node_index < LEAVES - 1).astype(jnp.float32)
        near_field = jnp.dot(kernel(own_pts, own_pts), cluster_test[node_index], precision=HIGHEST)
        near_field = near_field + weight_before * jnp.dot(kernel(own_pts, cluster_pts[before]), cluster_test[before], precision=HIGHEST)
        near_field = near_field + weight_after * jnp.dot(kernel(own_pts, cluster_pts[following]), cluster_test[following], precision=HIGHEST)
        residual = cluster_samp[node_index] - near_field
        pivots = leaf_pivots[node_index]
        picked = jnp.take(residual, pivots, axis=0)
        coeffs = solve_coeffs(picked)
        basis_rows = jnp.dot(residual, coeffs.T, precision=HIGHEST)
        projection = jnp.dot(coeffs, contract_rows(residual, cluster_test[node_index]), precision=HIGHEST)
        return (basis_rows, jnp.take(own_pts, pivots, axis=0), picked, projection)
    leaf_bases, skeleton, picked, projection = lax.map(leaf_node, jnp.arange(LEAVES, dtype=jnp.int32))

    def merge_level(tree_nodes, pivot_table, node_count):

        def merge_pair(node_index):
            first_node = tuple((member[2 * node_index] for member in tree_nodes))
            second_node = tuple((member[2 * node_index + 1] for member in tree_nodes))
            return combine(first_node, second_node, pivot_table[node_index])
        return lax.map(merge_pair, jnp.arange(node_count, dtype=jnp.int32))
    mid_bases, mid_nodes = merge_level((skeleton, picked, projection), mid_pivots, MIDS)
    top_bases, unused_nodes = merge_level(mid_nodes, top_pivots, TOPS)
    return (leaf_bases.reshape(NPTS, RANK), mid_bases.reshape(MIDS * 2 * RANK, RANK), top_bases.reshape(TOPS * 2 * RANK, RANK))
```

```python
import functools
import math

import jax
import jax.numpy as jnp
from jax import lax
from jax.experimental import pallas as pl
from jax.experimental.pallas import tpu as pltpu
from jax.sharding import PartitionSpec as P

DIM = 64
RANK = 256
SAMP = 512
BLK = 512
HALF = SAMP // 2
SIDE = 4
SCALE = math.log2(math.e) / DIM
HIGHEST = lax.Precision.HIGHEST
F32, BF16 = jnp.float32, jnp.bfloat16
VMEM = pltpu.VMEM


def along_x(k):
    return [(4 * x + y, 4 * ((x + k) % 4) + y) for x in range(4) for y in range(4)]


def along_y(k):
    return [(4 * x + y, 4 * x + (y + k) % 4) for x in range(4) for y in range(4)]


SIBLING = [(i, i ^ 1) for i in range(8)]
OUTER = [(1, 2), (2, 1), (3, 4), (4, 3), (5, 6), (6, 5)]
COUSIN = [(i, i ^ 2) for i in range(8)]


NN = (((1,), (0,)), ((), ()))
NT = (((1,), (1,)), ((), ()))


def mm(a, b, dims=NN):
    return lax.dot_general(a, b, dims, preferred_element_type=F32)


def split2(a):
    hi = a.astype(BF16)
    return hi, (a - hi.astype(F32)).astype(BF16)


def split3(a):
    hi = a.astype(BF16)
    rest = a - hi.astype(F32)
    mid = rest.astype(BF16)
    return hi, mid, (rest - mid.astype(F32)).astype(BF16)


def dot3(a, b, dims=NN):
    ah, al = split2(a)
    bh, bl = split2(b)
    return mm(ah, bh, dims) + (mm(ah, bl, dims) + mm(al, bh, dims))


def dot6(a, b, dims=NN):
    ah, am, al = split3(a)
    bh, bm, bl = split3(b)
    return mm(ah, bh, dims) + (
        (mm(ah, bm, dims) + mm(am, bh, dims))
        + (mm(am, bm, dims) + (mm(ah, bl, dims) + mm(al, bh, dims)))
    )


def pick(one_hot, a):
    h, m, l = split3(a)
    return (mm(one_hot, h) + mm(one_hot, m)) + mm(one_hot, l)


SHIFTS = (1, 3, 2)
LINE_X = (0, 1, 2, 3)
LINE_Y = (0, 4, 5, 6)
BLOCKS = 2 * SIDE - 1


def norm_rows(xt, first):
    rows = lax.broadcasted_iota(jnp.int32, (DIM, BLK), 0)
    sq = jnp.sum(xt * xt, axis=0, keepdims=True) * (-SCALE)
    h, m, l = (v.astype(F32) for v in split3(sq))
    one = jnp.ones_like(sq)
    aux = jnp.zeros((DIM, BLK), F32)
    for n, part in enumerate((h, m, l, one, one, one) if first else (one, one, one, h, m, l)):
        aux = jnp.where(rows == n, part, aux)
    return aux


def feature_kernel(points_ref, feat_ref):
    for i in range(BLOCKS):
        xt = points_ref[i * DIM:(i + 1) * DIM, :]
        scaled = xt * (2.0 * SCALE)
        hi = scaled.astype(BF16).astype(F32)
        feat = jnp.concatenate([hi, hi, scaled - hi, norm_rows(xt, True)], axis=0)
        feat_ref[i] = feat.T.astype(BF16)


def features(points_all):
    return pl.pallas_call(
        feature_kernel,
        out_shape=jax.ShapeDtypeStruct((BLOCKS, BLK, 4 * DIM), BF16),
        in_specs=[pl.BlockSpec(memory_space=VMEM)],
        out_specs=pl.BlockSpec(memory_space=VMEM),
        compiler_params=pltpu.CompilerParams(vmem_limit_bytes=32 * 2**20),
        cost_estimate=pl.CostEstimate(flops=10**9, bytes_accessed=3 * 2**20, transcendentals=0),
        name="features",
    )(points_all)


def near_kernel(plan, n_points, n_tests, weight_ref, feat_ref, *refs):
    refs = list(refs)
    points = [refs.pop(0) for _ in range(n_points)]
    tests = [refs.pop(0) for _ in range(n_tests)]
    before = [[refs.pop(0) for _ in g[0]] if g[2] else None for g in plan]
    outs = [[refs.pop(0) for _ in g[0]] for g in plan]
    buf_a, buf_b, *scratch = refs
    for n, (targets, sources, chained) in enumerate(plan):
        feat_t, feat_s, split_t, acc = scratch[4 * n:4 * n + 4]
        for i, target in enumerate(targets):
            feat_t[i] = feat_ref[target]
            acc[i] = before[n][i][...] if chained else jnp.zeros((BLK, HALF), F32)
        for b, (array, block, weighted, where, part, half) in enumerate(sources):
            xt = points[array][block * DIM:(block + 1) * DIM, :]
            hi, lo = split2(xt)
            feat_s[b, 0:DIM, :] = hi
            feat_s[b, DIM:2 * DIM, :] = lo
            feat_s[b, 2 * DIM:3 * DIM, :] = hi
            feat_s[b, 3 * DIM:, :] = norm_rows(xt, False).astype(BF16)
            test = tests[where][part * BLK:(part + 1) * BLK, half * HALF:(half + 1) * HALF]
            if weighted:
                test = test * weight_ref[0, 0]
            hi, lo = split2(test)
            split_t[b, 0:BLK, :] = hi
            split_t[b, BLK:2 * BLK, :] = hi
            split_t[b, 2 * BLK:, :] = lo
        count = len(sources)
        total = len(targets) * count

        def entries(t, buf):
            k = jnp.exp2(mm(feat_t[t // count], feat_s[t % count]))
            hi = k.astype(BF16)
            buf[:, 0:BLK] = hi
            buf[:, BLK:] = (k - hi.astype(F32)).astype(BF16)

        def fold(t, buf):
            b = t % count
            acc[t // count] += mm(buf[...], split_t[b, 0:2 * BLK, :]) + mm(
                buf[:, 0:BLK], split_t[b, 2 * BLK:, :]
            )

        entries(0, buf_a)

        @pl.loop(0, total // 2)
        def _(u):
            t = 2 * u
            entries(t + 1, buf_b)
            fold(t, buf_a)
            entries(jnp.minimum(t + 2, total - 1), buf_a)
            fold(t + 1, buf_b)

        if total % 2:
            fold(total - 1, buf_a)
        for i in range(len(targets)):
            outs[n][i][...] = acc[i]


def near(name, groups, tests, *, weight, feats, points):
    plan = [(t, src, acc is not None) for t, src, acc in groups]
    args = [weight, feats, *points, *tests]
    for _, _, acc in groups:
        args += acc or []
    n_out = sum(len(g[0]) for g in groups)
    work = sum(len(g[0]) * len(g[1]) for g in groups) * BLK * BLK
    scratch = [VMEM((BLK, 2 * BLK), BF16), VMEM((BLK, 2 * BLK), BF16)]
    for t, src, _ in groups:
        scratch += [
            VMEM((len(t), BLK, 4 * DIM), BF16),
            VMEM((len(src), 4 * DIM, BLK), BF16),
            VMEM((len(src), 3 * BLK, HALF), BF16),
            VMEM((len(t), BLK, HALF), F32),
        ]
    out = pl.pallas_call(
        functools.partial(near_kernel, plan, len(points), len(tests)),
        out_shape=[jax.ShapeDtypeStruct((BLK, HALF), F32)] * n_out,
        in_specs=[pl.BlockSpec(memory_space=pltpu.SMEM)]
        + [pl.BlockSpec(memory_space=VMEM)] * (len(args) - 1),
        out_specs=[pl.BlockSpec(memory_space=VMEM)] * n_out,
        scratch_shapes=scratch,
        compiler_params=pltpu.CompilerParams(vmem_limit_bytes=50 * 2**20),
        cost_estimate=pl.CostEstimate(
            flops=2 * work * (4 * DIM + 3 * HALF),
            bytes_accessed=4 * len(args) * BLK * HALF,
            transcendentals=work,
        ),
        name=name,
    )(*args)
    sums = []
    for t, _, _ in groups:
        sums.append(list(out[:len(t)]))
        out = out[len(t):]
    return sums


EXT = SAMP + 128


def resid_kernel(start_ref, piv_ref, samp_ref, points_ref, *refs):
    part_a, part_b = refs[:SIDE], refs[SIDE:2 * SIDE]
    resid_ref, picked_ref = refs[2 * SIDE:]
    near_a = (part_a[0][...] + part_a[1][...]) + (part_a[2][...] + part_a[3][...])
    near_b = (part_b[0][...] + part_b[1][...]) + (part_b[2][...] + part_b[3][...])
    resid_ref[:, :HALF] = samp_ref[:, :HALF] - near_a
    resid_ref[:, HALF:] = samp_ref[:, HALF:] - near_b
    column = lax.broadcasted_iota(jnp.int32, (RANK, BLK), 1) + start_ref[0, 0]
    one_hot = jnp.where(piv_ref[...] == column, 1.0, 0.0).astype(BF16)
    picked_ref[:, :SAMP] = pick(one_hot, resid_ref[...])
    skel = sum(mm(one_hot, part, NT) for part in split3(points_ref[...]))
    picked_ref[:, SAMP:] = jnp.concatenate([skel, jnp.zeros((RANK, EXT - SAMP - DIM), F32)], axis=1)


def vmem_call(kernel, outs, n_smem, n_vmem, scratch=(), name=None, flops=0):
    return pl.pallas_call(
        kernel,
        out_shape=[jax.ShapeDtypeStruct(s, F32) for s in outs],
        in_specs=[pl.BlockSpec(memory_space=pltpu.SMEM)] * n_smem
        + [pl.BlockSpec(memory_space=VMEM)] * n_vmem,
        out_specs=[pl.BlockSpec(memory_space=VMEM)] * len(outs),
        scratch_shapes=list(scratch),
        compiler_params=pltpu.CompilerParams(vmem_limit_bytes=48 * 2**20),
        cost_estimate=pl.CostEstimate(flops=flops, bytes_accessed=4 * 2**20, transcendentals=0),
        name=name,
    )


SOLVE_SCRATCH = [VMEM((RANK, RANK), F32), VMEM((RANK, RANK), F32)]


def inverse_gram(picked, err_ref, inv_ref):
    gram = dot6(picked, picked, NT)
    eye = (
        lax.broadcasted_iota(jnp.int32, (RANK, RANK), 0)
        == lax.broadcasted_iota(jnp.int32, (RANK, RANK), 1)
    ).astype(F32)
    shift = jnp.sum(gram * eye) / RANK + 1e-06
    gram = gram + shift * eye
    bound = jnp.max(jnp.sum(jnp.abs(gram), axis=0, keepdims=True))
    alpha = 2.0 / (jnp.full((1, 1), 1.0, F32) * (bound + shift))
    err_ref[...] = eye - alpha * gram
    inv_ref[...] = alpha * eye

    def step(state):
        n, _ = state
        err = err_ref[...]
        eh, el = split2(err)
        ih, il = split2(inv_ref[...])
        inv_ref[...] += mm(ih, eh) + (mm(ih, el) + mm(il, eh))
        sq = mm(eh, eh) + (mm(eh, el) + mm(el, eh))
        err_ref[...] = sq
        return n + 1, jnp.sum(sq * sq)

    lax.while_loop(lambda st: (st[0] < 24) & (st[1] > 1e-6), step, (jnp.int32(0), jnp.float32(1e9)))
    for _ in range(2):
        inv = inv_ref[...]
        inv_ref[...] = inv + dot3(inv, eye - dot6(gram, inv))
    return inv_ref[...]


def leaf_kernel(resid_ref, test_ref, picked_ref, basis_ref, proj_ref, err_ref, inv_ref):
    picked = picked_ref[:, :SAMP]
    coeffs = dot3(inverse_gram(picked, err_ref, inv_ref), picked)
    resid = resid_ref[...]
    basis_ref[...] = dot3(resid, coeffs, NT)
    proj_ref[...] = dot3(dot3(coeffs, resid, NT), test_ref[...])


def coupling(a, b):
    def norm3(v):
        return split3(v * v)

    ones = jnp.ones((RANK, DIM), BF16)
    inner = dot6(a, b, NT)
    na = sum(mm(p, ones, NT) for p in norm3(a))
    nb = sum(mm(ones, p, NT) for p in norm3(b))
    return jnp.exp2(-SCALE * (na + nb - 2.0 * inner))


def merge_kernel(top, share, info_ref, piv_ref, *refs):
    if top:
        pick_own, proj_own, first, other, share_ref, stack_ref, err_ref, inv_ref = refs
        core0 = info_ref[0, 2] == 0
        peer_pick = jnp.where(core0, first[...], other[...])
        peer_proj = jnp.where(core0, other[:, :SAMP], first[:, :SAMP])
    else:
        (pick_own, proj_own, pick_peer, proj_peer) = refs[:4]
        (share_ref, picked_ref, proj_ref, send_ref, stack_ref, err_ref, inv_ref) = refs[4:]
        peer_pick, peer_proj = pick_peer[...], proj_peer[...]
    lower = info_ref[0, 0] == 0

    def order(own, peer):
        return jnp.where(lower, own, peer), jnp.where(lower, peer, own)

    pick_a, pick_b = order(pick_own[...], peer_pick)
    proj_a, proj_b = order(proj_own[...], peer_proj)
    skel_a, skel_b = pick_a[:, SAMP:SAMP + DIM], pick_b[:, SAMP:SAMP + DIM]
    stack_ref[0:RANK, :SAMP] = pick_a[:, :SAMP] - dot3(coupling(skel_a, skel_b), proj_b)
    stack_ref[RANK:, :SAMP] = pick_b[:, :SAMP] - dot3(coupling(skel_b, skel_a), proj_a)
    stack_ref[0:RANK, SAMP:] = pick_a[:, SAMP:]
    stack_ref[RANK:, SAMP:] = pick_b[:, SAMP:]
    one_hot = jnp.where(
        piv_ref[...] == lax.broadcasted_iota(jnp.int32, (RANK, 2 * RANK), 1), 1.0, 0.0
    ).astype(BF16)
    picked_all = pick(one_hot, stack_ref[...])
    picked = picked_all[:, :SAMP]
    coeffs = dot3(inverse_gram(picked, err_ref, inv_ref), picked)
    rows = stack_ref[pl.ds(pl.multiple_of(info_ref[0, 1], 8), share), :SAMP]
    share_ref[...] = dot3(rows, coeffs, NT)
    if not top:
        picked_ref[...] = picked_all
        basis_t = dot3(coeffs, stack_ref[:, :SAMP], NT)
        proj = dot3(basis_t[:, :RANK], proj_a) + dot3(basis_t[:, RANK:], proj_b)
        proj_ref[...] = proj
        send_ref[:, :SAMP] = jnp.where(lower, picked, proj)
        send_ref[:, SAMP:] = picked_all[:, SAMP:]


def merge(top, share, info, pivots, *node):
    outs = [(share, RANK)] if top else [(share, RANK), (RANK, EXT), (RANK, SAMP), (RANK, EXT)]
    return vmem_call(
        functools.partial(merge_kernel, top, share),
        outs, 1, 5,
        [VMEM((2 * RANK, EXT), F32), *SOLVE_SCRATCH],
        name="merge_top" if top else "merge_mid",
        flops=3 * 10**9,
    )(info, pivots.reshape(RANK, 1), *node)


def sum_row(part):
    share = part.shape[0] // 16
    parts = lax.all_to_all(part.reshape(16, share, -1), "row", 0, 0)
    mine = jnp.sum(parts, axis=0)
    every = lax.all_to_all(jnp.broadcast_to(mine[None], (16, share, mine.shape[1])), "row", 0, 0)
    return every.reshape(part.shape)


def body(points, samples, test_matrix, near_mask, leaf_pivots, mid_pivots, top_pivots):
    leaf = lax.axis_index("leaf")
    row = lax.axis_index("row")
    core = leaf & 1
    xt = points.T
    x_line = [lax.ppermute(xt, "row", along_x(k)) for k in SHIFTS]
    y_line = [lax.ppermute(xt, "row", along_y(k)) for k in SHIFTS]
    pts = jnp.concatenate([xt, *x_line, *y_line], axis=0)
    pts_sib = lax.ppermute(pts, "leaf", SIBLING)
    pts_out = lax.ppermute(pts, "leaf", OUTER)
    points_all = [pts, pts_sib, pts_out]

    weight = jnp.where(core == 0, near_mask[0, 0], near_mask[0, 1]).astype(F32).reshape(1, 1)
    feats = features(pts)
    run = functools.partial(near, weight=weight, feats=feats, points=points_all)

    test_sib = lax.ppermute(test_matrix, "leaf", SIBLING)
    test_out = lax.ppermute(test_matrix, "leaf", OUTER)
    test_a, test_b = test_matrix[:, :HALF], test_matrix[:, HALF:]
    far = {("a", k): lax.ppermute(test_a, "row", along_x(k)) for k in (2, 1, 3)}
    far.update({("b", k): lax.ppermute(test_b, "row", along_y(k)) for k in (2, 1)})

    part_a, part_b = run("near_local", [
        (LINE_Y, [(n, 0, n == 2, n, 0, 0) for n in range(3)], None),
        (LINE_X, [(n, 0, n == 2, n, 0, 1) for n in range(3)], None),
    ], [test_matrix, test_sib, test_out])

    late, far, part_a, part_b = lax.optimization_barrier((test_b, far, part_a, part_b))
    far["b", 3] = lax.ppermute(late, "row", along_y(3))
    line_a = [jnp.concatenate([far["a", k] for k in SHIFTS], axis=0)]
    line_b = [jnp.concatenate([far["b", k] for k in SHIFTS], axis=0)]
    for line in (line_a, line_b):
        line.append(lax.ppermute(line[0], "leaf", SIBLING))
        line.append(lax.ppermute(line[0], "leaf", OUTER))

    def sources(line, arrays, first=0):
        return [(n, line[p + 1], n == 2, first + n - arrays[0], p, 0) for n in arrays for p in range(3)]

    (far_a,) = run("near_a", [(LINE_Y[1:], sources(LINE_X, (0, 1)), part_a[1:])], line_a[:2])
    (far_b,) = run("near_b", [(LINE_X[1:], sources(LINE_Y, (0, 1)), part_b[1:])], line_b[:2])
    (far_a,) = run("near_outer_a", [(LINE_Y[1:], sources(LINE_X, (2,)), far_a)], line_a[2:])
    got_a = [lax.ppermute(v, "row", along_y(-k)) for v, k in zip(far_a, SHIFTS)]
    (far_b,) = run("near_outer_b", [(LINE_X[1:], sources(LINE_Y, (2,)), far_b)], line_b[2:])
    got_b = [lax.ppermute(v, "row", along_x(-k)) for v, k in zip(far_b, SHIFTS)]
    own_a, own_b = run("near_own", [
        ((0,), sources(LINE_X, (0, 1, 2)), part_a[:1]),
        ((0,), sources(LINE_Y, (0, 1, 2), 3), part_b[:1]),
    ], line_a + line_b)

    pivots = leaf_pivots[0]
    resid, picked = vmem_call(
        resid_kernel, [(BLK, SAMP), (RANK, EXT)], 1, 3 + 2 * SIDE, name="residual", flops=10**9
    )((row * BLK).reshape(1, 1), pivots.reshape(RANK, 1), samples, xt, *own_a, *got_a, *own_b, *got_b)
    picked = sum_row(picked)
    picked_sib = lax.ppermute(picked, "leaf", SIBLING)
    leaf_basis, proj = vmem_call(
        leaf_kernel, [(BLK, RANK), (RANK, SAMP)], 0, 3, SOLVE_SCRATCH, name="leaf", flops=3 * 10**9
    )(resid, test_matrix, picked)
    proj = sum_row(proj)
    proj_sib = lax.ppermute(proj, "leaf", SIBLING)

    def info(lower, first):
        return jnp.stack([lower, first, core]).astype(jnp.int32).reshape(1, 3)

    mid_row = lax.dynamic_index_in_dim(mid_pivots, leaf >> 1, 0, keepdims=False)
    top_row = lax.dynamic_index_in_dim(top_pivots, leaf >> 2, 0, keepdims=False)
    mid_share, top_share = RANK // 16, RANK // 32
    mid_basis, picked, proj, send = merge(
        False, mid_share, info(core, core * RANK + row * mid_share), mid_row,
        picked, proj, picked_sib, proj_sib,
    )
    first = lax.ppermute(send, "leaf", COUSIN)
    other = lax.ppermute(first, "leaf", SIBLING)
    second = leaf >> 1 & 1
    (top_basis,) = merge(
        True, top_share, info(second, second * RANK + core * (RANK // 2) + row * top_share), top_row,
        picked, proj, first, other,
    )
    return (leaf_basis, mid_basis, top_basis)


def solution(mesh):
    split = P(("leaf", "row"), None)
    return jax.shard_map(
        body,
        mesh=mesh,
        in_specs=(split, split, split, P("leaf", None), P("leaf", None), P(), P()),
        out_specs=(split, split, split),
        check_vma=False,
    )
```

```python
import functools
import math

import jax
import jax.numpy as jnp
from jax import lax
from jax.experimental import pallas as pl
from jax.experimental.pallas import tpu as pltpu
from jax.sharding import PartitionSpec as P

DIM = 64
RANK = 256
SAMP = 512
BLK = 512
SIDE = 4
SCALE = math.log2(math.e) / DIM
HIGHEST = lax.Precision.HIGHEST
F32, BF16 = jnp.float32, jnp.bfloat16
VMEM = pltpu.VMEM


def along_x(k):
    return [(4 * x + y, 4 * ((x + k) % 4) + y) for x in range(4) for y in range(4)]


def along_y(k):
    return [(4 * x + y, 4 * x + (y + k) % 4) for x in range(4) for y in range(4)]


SIBLING = [(i, i ^ 1) for i in range(8)]
OUTER = [(1, 2), (2, 1), (3, 4), (4, 3), (5, 6), (6, 5)]
COUSIN = [(i, i ^ 2) for i in range(8)]


NN = (((1,), (0,)), ((), ()))
NT = (((1,), (1,)), ((), ()))


def mm(a, b, dims=NN):
    return lax.dot_general(a, b, dims, preferred_element_type=F32)


def split2(a):
    hi = a.astype(BF16)
    return hi, (a - hi.astype(F32)).astype(BF16)


def split3(a):
    hi = a.astype(BF16)
    rest = a - hi.astype(F32)
    mid = rest.astype(BF16)
    return hi, mid, (rest - mid.astype(F32)).astype(BF16)


def dot3(a, b, dims=NN):
    ah, al = split2(a)
    bh, bl = split2(b)
    return mm(ah, bh, dims) + (mm(ah, bl, dims) + mm(al, bh, dims))


def dot6(a, b, dims=NN):
    ah, am, al = split3(a)
    bh, bm, bl = split3(b)
    return mm(ah, bh, dims) + (
        (mm(ah, bm, dims) + mm(am, bh, dims))
        + (mm(am, bm, dims) + (mm(ah, bl, dims) + mm(al, bh, dims)))
    )


def pick(one_hot, a):
    h, m, l = split3(a)
    return (mm(one_hot, h) + mm(one_hot, m)) + mm(one_hot, l)


SHIFTS = (1, 3, 2)
MSG0, MSG1, MSG2 = BLK + DIM, 2 * (BLK + DIM), BLK + DIM
PLACES = ((0, 0, BLK), (1, 0, 2 * BLK), (1, BLK, 2 * BLK + DIM), (2, 0, BLK))
COUNT = 3 * SIDE


def norm_rows(xt, first):
    rows = lax.broadcasted_iota(jnp.int32, (DIM, BLK), 0)
    sq = jnp.sum(xt * xt, axis=0, keepdims=True) * (-SCALE)
    h, m, l = (v.astype(F32) for v in split3(sq))
    one = jnp.ones_like(sq)
    aux = jnp.zeros((DIM, BLK), F32)
    for n, part in enumerate((h, m, l, one, one, one) if first else (one, one, one, h, m, l)):
        aux = jnp.where(rows == n, part, aux)
    return aux


def left_features(xt):
    scaled = xt * (2.0 * SCALE)
    hi = scaled.astype(BF16).astype(F32)
    feat = jnp.concatenate([hi, hi, scaled - hi, norm_rows(xt, True)], axis=0)
    return feat.T.astype(BF16)


def right_features(xt, ref):
    hi, lo = split2(xt)
    ref[0:DIM, :] = hi
    ref[DIM:2 * DIM, :] = lo
    ref[2 * DIM:3 * DIM, :] = hi
    ref[3 * DIM:, :] = norm_rows(xt, False).astype(BF16)


def pivot_kernel(
    info_ref, weight_ref, piv_ref, all_ref, samp_ref, own_ref, sib_ref, out_ref,
    feat_ref, part_ref, skel_ref, right_ref
):
    row = info_ref[0, 0]
    x, y = row >> 2, row & 3
    for i, k in enumerate((0,) + SHIFTS):
        feat_ref[i] = left_features(all_ref[x << 2 | (y + SIDE - k & 3)])
    column = lax.broadcasted_iota(jnp.int32, (RANK, BLK), 1)
    piv = piv_ref[...]

    def rows_of(r):
        return jnp.where(piv == column + r * BLK, 1.0, 0.0).astype(BF16)

    got = jnp.zeros((RANK, 3 * DIM), F32)
    for r in range(16):
        got += mm(rows_of(r), jnp.concatenate(split3(all_ref[r]), axis=0), NT)
    skel = (got[:, :DIM] + got[:, DIM:2 * DIM]) + got[:, 2 * DIM:]
    skel_ref[...] = jnp.concatenate([skel, jnp.zeros((RANK, DIM), F32)], axis=1)
    scaled = skel * (2.0 * SCALE)
    hi = scaled.astype(BF16).astype(F32)
    lane = lax.broadcasted_iota(jnp.int32, (RANK, DIM), 1)
    sq = jnp.sum(skel * skel, axis=1, keepdims=True) * (-SCALE)
    aux = jnp.where(lane < 6, 1.0, 0.0)
    for n, part in enumerate(split3(sq)):
        aux = jnp.where(lane == n, part.astype(F32), aux)
    feat = jnp.concatenate([hi, hi, scaled - hi, aux], axis=1).astype(BF16)
    total = pick(rows_of(row), samp_ref[...])
    for n, ref in enumerate((own_ref, sib_ref, out_ref)):
        right_features(ref[BLK:, :], right_ref)
        kern = jnp.exp2(mm(feat, right_ref[...]))
        if n == 2:
            kern = kern * weight_ref[0, 0]
        total -= dot3(kern, ref[0:BLK, :])
    part_ref[...] = total


def weights_kernel(weight_ref, coeffs_ref, *refs):
    msgs = [refs[3 * n:3 * n + 3] for n in range(3)]
    prod_ref, right_ref = refs[9:]
    ch, cl = split2(coeffs_ref[...])
    for n in range(3):
        for p, (m, first, point) in enumerate(PLACES):
            ref, at = msgs[n][m], n * SIDE + p
            right_features(ref[point:point + DIM, :], right_ref.at[at])
            test = ref[first:first + BLK, :]
            if n == 2:
                test = test * weight_ref[0, 0]
            th, tl = split2(test)
            hi, lo = split2(mm(th, ch, NT) + (mm(th, cl, NT) + mm(tl, ch, NT)))
            prod_ref[at, 0:BLK, :] = hi
            prod_ref[at, BLK:, :] = lo


def near_kernel(targets, feat_ref, prod_ref, right_ref, *refs):
    outs, (acc, buf_a, buf_b) = refs[:len(targets)], refs[len(targets):]
    acc[...] = jnp.zeros_like(acc)
    total = len(targets) * COUNT

    def left(t):
        i = t // COUNT
        return feat_ref[targets[0] + i * (targets[-1] - targets[0])]

    def entries(t, buf):
        k = jnp.exp2(mm(left(t), right_ref[t % COUNT]))
        hi = k.astype(BF16)
        buf[:, BLK:] = hi
        buf[:, 0:BLK] = (k - hi.astype(F32)).astype(BF16)

    def fold(t, buf):
        b = t % COUNT
        acc[t // COUNT] += mm(buf[...], prod_ref[b]) + mm(buf[:, BLK:], prod_ref[b, 0:BLK, :])

    entries(0, buf_a)

    @pl.loop(0, total // 2)
    def _(u):
        t = 2 * u
        entries(t + 1, buf_b)
        fold(t, buf_a)
        entries(jnp.minimum(t + 2, total - 1), buf_a)
        fold(t + 1, buf_b)

    for i in range(len(targets)):
        outs[i][...] = acc[i]


def call(kernel, outs, n_smem, n_vmem, scratch=(), name=None, flops=0, trans=0):
    return pl.pallas_call(
        kernel,
        out_shape=[jax.ShapeDtypeStruct(s, t) for s, t in outs],
        in_specs=[pl.BlockSpec(memory_space=pltpu.SMEM)] * n_smem
        + [pl.BlockSpec(memory_space=VMEM)] * n_vmem,
        out_specs=[pl.BlockSpec(memory_space=VMEM)] * len(outs),
        scratch_shapes=list(scratch),
        compiler_params=pltpu.CompilerParams(vmem_limit_bytes=50 * 2**20),
        cost_estimate=pl.CostEstimate(flops=flops, bytes_accessed=4 * 2**20, transcendentals=trans),
        name=name,
    )


def near(targets, feats, prods, rights):
    return call(
        functools.partial(near_kernel, targets),
        [((BLK, RANK), F32)] * len(targets), 0, 3,
        [VMEM((len(targets), BLK, RANK), F32), VMEM((BLK, 2 * BLK), BF16), VMEM((BLK, 2 * BLK), BF16)],
        name="near", flops=10**6, trans=0,
    )(feats, prods, rights)


SOLVE_SCRATCH = [VMEM((RANK, RANK), F32), VMEM((RANK, RANK), F32)]


def inverse_gram(picked, err_ref, inv_ref):
    gram = dot6(picked, picked, NT)
    eye = (
        lax.broadcasted_iota(jnp.int32, (RANK, RANK), 0)
        == lax.broadcasted_iota(jnp.int32, (RANK, RANK), 1)
    ).astype(F32)
    shift = jnp.sum(gram * eye) / RANK + 1e-06
    gram = gram + shift * eye
    bound = jnp.max(jnp.sum(jnp.abs(gram), axis=0, keepdims=True))
    alpha = 2.0 / (jnp.full((1, 1), 1.0, F32) * (bound + shift))
    err_ref[...] = eye - alpha * gram
    inv_ref[...] = alpha * eye

    def step(state):
        n, _ = state
        err = err_ref[...]
        eh, el = split2(err)
        ih, il = split2(inv_ref[...])
        inv_ref[...] += mm(ih, eh) + (mm(ih, el) + mm(il, eh))
        sq = mm(eh, eh) + (mm(eh, el) + mm(el, eh))
        err_ref[...] = sq
        return n + 1, jnp.sum(sq * sq)

    lax.while_loop(lambda st: (st[0] < 24) & (st[1] > 1e-6), step, (jnp.int32(0), jnp.float32(1e9)))
    for _ in range(2):
        inv = inv_ref[...]
        inv_ref[...] = inv + dot3(inv, eye - dot6(gram, inv))
    return inv_ref[...]


def solve_kernel(picked_ref, coeffs_ref, err_ref, inv_ref):
    picked = picked_ref[...]
    coeffs_ref[...] = dot3(inverse_gram(picked, err_ref, inv_ref), picked)


def basis_kernel(samp_ref, test_ref, coeffs_ref, *refs):
    parts, (basis_ref, proj_ref) = refs[:SIDE], refs[SIDE:]
    near_field = (parts[0][...] + parts[1][...]) + (parts[2][...] + parts[3][...])
    basis = dot3(samp_ref[...], coeffs_ref[...], NT) - near_field
    basis_ref[...] = basis
    proj_ref[...] = dot3(basis.T, test_ref[...])


def coupling(a, b):
    def norm3(v):
        return split3(v * v)

    ones = jnp.ones((RANK, DIM), BF16)
    inner = dot6(a, b, NT)
    na = sum(mm(p, ones, NT) for p in norm3(a))
    nb = sum(mm(ones, p, NT) for p in norm3(b))
    return jnp.exp2(-SCALE * (na + nb - 2.0 * inner))


EXT = SAMP + 2 * DIM


def merge_kernel(top, share, info_ref, piv_ref, *refs):
    if top:
        pick_ref, skel_ref, proj_own, first, other, share_ref, stack_ref, err_ref, inv_ref = refs
        core0 = info_ref[0, 2] == 0
        peer_pick = jnp.where(core0, first[:, :SAMP], other[:, :SAMP])
        peer_proj = jnp.where(core0, other[:, :SAMP], first[:, :SAMP])
        peer_skel = first[:, SAMP:]
    else:
        (pick_ref, skel_ref, proj_own, pick_peer, skel_peer, proj_peer) = refs[:6]
        (share_ref, picked_ref, skel_out, proj_ref, send_ref, stack_ref, err_ref, inv_ref) = refs[6:]
        peer_pick, peer_proj, peer_skel = pick_peer[...], proj_peer[...], skel_peer[...]
    lower = info_ref[0, 0] == 0

    def order(own, peer):
        return jnp.where(lower, own, peer), jnp.where(lower, peer, own)

    pick_a, pick_b = order(pick_ref[...], peer_pick)
    proj_a, proj_b = order(proj_own[...], peer_proj)
    skel_a, skel_b = order(skel_ref[...], peer_skel)
    stack_ref[0:RANK, :SAMP] = pick_a - dot3(coupling(skel_a[:, :DIM], skel_b[:, :DIM]), proj_b)
    stack_ref[RANK:, :SAMP] = pick_b - dot3(coupling(skel_b[:, :DIM], skel_a[:, :DIM]), proj_a)
    stack_ref[0:RANK, SAMP:] = skel_a
    stack_ref[RANK:, SAMP:] = skel_b
    one_hot = jnp.where(
        piv_ref[...] == lax.broadcasted_iota(jnp.int32, (RANK, 2 * RANK), 1), 1.0, 0.0
    ).astype(BF16)
    picked_all = pick(one_hot, stack_ref[...])
    picked = picked_all[:, :SAMP]
    coeffs = dot3(inverse_gram(picked, err_ref, inv_ref), picked)
    rows = stack_ref[pl.ds(pl.multiple_of(info_ref[0, 1], 8), share), :SAMP]
    share_ref[...] = dot3(rows, coeffs, NT)
    if not top:
        picked_ref[...] = picked
        skel_out[...] = picked_all[:, SAMP:]
        basis_t = dot3(coeffs, stack_ref[:, :SAMP], NT)
        proj = dot3(basis_t[:, :RANK], proj_a) + dot3(basis_t[:, RANK:], proj_b)
        proj_ref[...] = proj
        send_ref[:, :SAMP] = jnp.where(lower, picked, proj)
        send_ref[:, SAMP:] = picked_all[:, SAMP:]


def merge(top, share, info, pivots, *node):
    outs = [(share, RANK)]
    if not top:
        outs += [(RANK, SAMP), (RANK, 2 * DIM), (RANK, SAMP), (RANK, EXT)]
    return call(
        functools.partial(merge_kernel, top, share),
        [(o, F32) for o in outs], 1, 1 + len(node),
        [VMEM((2 * RANK, EXT), F32), *SOLVE_SCRATCH],
        name="merge_top" if top else "merge_mid",
        flops=3 * 10**9,
    )(info, pivots.reshape(RANK, 1), *node)


def every_row(part):
    return lax.all_to_all(jnp.broadcast_to(part[None], (16, *part.shape)), "row", 0, 0)


def sum_row(part, between=None):
    share = part.shape[0] // 16
    parts = lax.all_to_all(part.reshape(16, share, -1), "row", 0, 0)
    mine = jnp.sum(parts, axis=0)
    if between is not None:
        mine, between = lax.optimization_barrier((mine, between))
    return every_row(mine).reshape(part.shape), between


def body(points, samples, test_matrix, near_mask, leaf_pivots, mid_pivots, top_pivots):
    leaf = lax.axis_index("leaf")
    row = lax.axis_index("row")
    core, x, y = leaf & 1, row >> 2, row & 3
    xt = points.T
    pivots = leaf_pivots[0].reshape(RANK, 1)
    weight = jnp.where(core == 0, near_mask[0, 0], near_mask[0, 1]).astype(F32).reshape(1, 1)

    def relay(message):
        return [message, lax.ppermute(message, "leaf", SIBLING), lax.ppermute(message, "leaf", OUTER)]

    message_0 = relay(jnp.concatenate([test_matrix, xt], axis=0))
    test_1 = lax.ppermute(test_matrix, "row", along_x(1))
    test_3 = lax.ppermute(test_matrix, "row", along_x(3))
    points_all = every_row(xt)

    def points_from(k):
        return lax.dynamic_index_in_dim(points_all, (x + SIDE - k & 3) << 2 | y, 0, keepdims=False)

    feats, part, skel = call(
        pivot_kernel,
        [((SIDE, BLK, 4 * DIM), BF16), ((RANK, SAMP), F32), ((RANK, 2 * DIM), F32)], 2, 6,
        [VMEM((4 * DIM, BLK), BF16)], name="pivot", flops=3 * 10**9,
    )(row.reshape(1, 1), weight, pivots, points_all, samples, *message_0)
    late, part, test_1, test_3 = lax.optimization_barrier((test_matrix, part, test_1, test_3))
    test_2 = lax.ppermute(late, "row", along_x(2))
    message_1 = jnp.concatenate([test_1, test_3, points_from(1), points_from(3)], axis=0)
    message_1, part = lax.optimization_barrier((message_1, part))
    message_1 = relay(message_1)
    message_2 = jnp.concatenate([test_2, points_from(2)], axis=0)
    picked, message_2 = sum_row(part, message_2)
    message_2 = relay(message_2)
    (coeffs,) = call(
        solve_kernel, [((RANK, SAMP), F32)], 0, 1, SOLVE_SCRATCH, name="solve", flops=3 * 10**9
    )(picked)
    picked_sib = lax.ppermute(picked, "leaf", SIBLING)
    skel_sib = lax.ppermute(skel, "leaf", SIBLING)

    messages = [m[n] for n in range(3) for m in (message_0, message_1, message_2)]
    prods, rights = call(
        weights_kernel,
        [((COUNT, 2 * BLK, RANK), BF16), ((COUNT, 4 * DIM, BLK), BF16)], 1, 10,
        name="weights", flops=6 * 10**9,
    )(weight, coeffs, *messages)
    (sum_2,) = near((3,), feats, prods, rights)
    sum_2 = lax.ppermute(sum_2, "row", along_y(-2))
    sum_1, sum_3 = near((1, 2), feats, prods, rights)
    sum_1 = lax.ppermute(sum_1, "row", along_y(-1))
    sum_3 = lax.ppermute(sum_3, "row", along_y(-3))
    (sum_0,) = near((0,), feats, prods, rights)
    leaf_basis, proj = call(
        basis_kernel, [((BLK, RANK), F32), ((RANK, SAMP), F32)], 0, 3 + SIDE, name="basis", flops=10**9
    )(samples, test_matrix, coeffs, sum_0, sum_1, sum_2, sum_3)
    proj, _ = sum_row(proj)
    proj_sib = lax.ppermute(proj, "leaf", SIBLING)

    def info(lower, first):
        return jnp.stack([lower, first, core]).astype(jnp.int32).reshape(1, 3)

    mid_row = lax.dynamic_index_in_dim(mid_pivots, leaf >> 1, 0, keepdims=False)
    top_row = lax.dynamic_index_in_dim(top_pivots, leaf >> 2, 0, keepdims=False)
    mid_share, top_share = RANK // 16, RANK // 32
    mid_basis, picked, skel, proj, send = merge(
        False, mid_share, info(core, core * RANK + row * mid_share), mid_row,
        picked, skel, proj, picked_sib, skel_sib, proj_sib,
    )
    first = lax.ppermute(send, "leaf", COUSIN)
    other = lax.ppermute(first, "leaf", SIBLING)
    second = leaf >> 1 & 1
    (top_basis,) = merge(
        True, top_share, info(second, second * RANK + core * (RANK // 2) + row * top_share), top_row,
        picked, skel, proj, first, other,
    )
    return (leaf_basis, mid_basis, top_basis)


def solution(mesh):
    split = P(("leaf", "row"), None)
    return jax.shard_map(
        body,
        mesh=mesh,
        in_specs=(split, split, split, P("leaf", None), P("leaf", None), P(), P()),
        out_specs=(split, split, split),
        check_vma=False,
    )
```

```python
import functools
import math

import jax
import jax.numpy as jnp
from jax import lax
from jax.experimental import pallas as pl
from jax.experimental.pallas import tpu as pltpu
from jax.sharding import PartitionSpec as P

DIM = 64
RANK = 256
SAMP = 512
BLK = 512
SIDE = 4
SCALE = math.log2(math.e) / DIM
HIGHEST = lax.Precision.HIGHEST
F32, BF16 = jnp.float32, jnp.bfloat16
VMEM = pltpu.VMEM


def along_x(k):
    return [(4 * x + y, 4 * ((x + k) % 4) + y) for x in range(4) for y in range(4)]


def along_y(k):
    return [(4 * x + y, 4 * x + (y + k) % 4) for x in range(4) for y in range(4)]


SIBLING = [(i, i ^ 1) for i in range(8)]
OUTER = [(1, 2), (2, 1), (3, 4), (4, 3), (5, 6), (6, 5)]
COUSIN = [(i, i ^ 2) for i in range(8)]


NN = (((1,), (0,)), ((), ()))
NT = (((1,), (1,)), ((), ()))


def mm(a, b, dims=NN):
    return lax.dot_general(a, b, dims, preferred_element_type=F32)


def split2(a):
    hi = a.astype(BF16)
    return hi, (a - hi.astype(F32)).astype(BF16)


def split3(a):
    hi = a.astype(BF16)
    rest = a - hi.astype(F32)
    mid = rest.astype(BF16)
    return hi, mid, (rest - mid.astype(F32)).astype(BF16)


def dot3(a, b, dims=NN):
    ah, al = split2(a)
    bh, bl = split2(b)
    return mm(ah, bh, dims) + (mm(ah, bl, dims) + mm(al, bh, dims))


def dot6(a, b, dims=NN):
    ah, am, al = split3(a)
    bh, bm, bl = split3(b)
    return mm(ah, bh, dims) + (
        (mm(ah, bm, dims) + mm(am, bh, dims))
        + (mm(am, bm, dims) + (mm(ah, bl, dims) + mm(al, bh, dims)))
    )


def pick(one_hot, a):
    h, m, l = split3(a)
    return (mm(one_hot, h) + mm(one_hot, m)) + mm(one_hot, l)


SHIFTS = (1, 3, 2)
COUNT = 3 * SIDE


def norm_rows(xt, first):
    rows = lax.broadcasted_iota(jnp.int32, (DIM, BLK), 0)
    sq = jnp.sum(xt * xt, axis=0, keepdims=True) * (-SCALE)
    h, m, l = (v.astype(F32) for v in split3(sq))
    one = jnp.ones_like(sq)
    aux = jnp.zeros((DIM, BLK), F32)
    for n, part in enumerate((h, m, l, one, one, one) if first else (one, one, one, h, m, l)):
        aux = jnp.where(rows == n, part, aux)
    return aux


def left_features(xt):
    scaled = xt * (2.0 * SCALE)
    hi = scaled.astype(BF16).astype(F32)
    feat = jnp.concatenate([hi, hi, scaled - hi, norm_rows(xt, True)], axis=0)
    return feat.T.astype(BF16)


def right_features(xt, ref):
    hi, lo = split2(xt)
    ref[0:DIM, :] = hi
    ref[DIM:2 * DIM, :] = lo
    ref[2 * DIM:3 * DIM, :] = hi
    ref[3 * DIM:, :] = norm_rows(xt, False).astype(BF16)


def rows_of(start, piv_ref):
    column = lax.broadcasted_iota(jnp.int32, (RANK, BLK), 1)
    return jnp.where(piv_ref[...] == column + start, 1.0, 0.0).astype(BF16)


def skel_kernel(start_ref, piv_ref, points_ref, skel_ref):
    one_hot = rows_of(start_ref[0, 0], piv_ref)
    skel = sum(mm(one_hot, part, NT) for part in split3(points_ref[...]))
    skel_ref[...] = jnp.concatenate([skel, jnp.zeros((RANK, DIM), F32)], axis=1)


def feature_kernel(p0, p1, p2, p3, feat_ref):
    for i, ref in enumerate((p0, p1, p2, p3)):
        feat_ref[i] = left_features(ref[...])


def pivot_kernel(
    start_ref, weight_ref, piv_ref, skel_ref, samp_ref, own_ref, sib_ref, out_ref, part_ref, right_ref
):
    skel = skel_ref[:, :DIM]
    scaled = skel * (2.0 * SCALE)
    hi = scaled.astype(BF16).astype(F32)
    lane = lax.broadcasted_iota(jnp.int32, (RANK, DIM), 1)
    sq = jnp.sum(skel * skel, axis=1, keepdims=True) * (-SCALE)
    aux = jnp.where(lane < 6, 1.0, 0.0)
    for n, part in enumerate(split3(sq)):
        aux = jnp.where(lane == n, part.astype(F32), aux)
    feat = jnp.concatenate([hi, hi, scaled - hi, aux], axis=1).astype(BF16)
    total = pick(rows_of(start_ref[0, 0], piv_ref), samp_ref[...])
    for n, ref in enumerate((own_ref, sib_ref, out_ref)):
        right_features(ref[BLK:, :], right_ref)
        kern = jnp.exp2(mm(feat, right_ref[...]))
        if n == 2:
            kern = kern * weight_ref[0, 0]
        total -= dot3(kern, ref[0:BLK, :])
    part_ref[...] = total


def far_kernel(targets, weight_ref, coeffs_ref, feat_ref, *refs):
    msgs, refs = refs[:COUNT], refs[COUNT:]
    outs, (prod_ref, right_ref), scratch = refs[:len(targets)], refs[len(targets):-3], refs[-3:]
    ch, cl = split2(coeffs_ref[...])
    for at, ref in enumerate(msgs):
        right_features(ref[BLK:, :], right_ref.at[at])
        test = ref[0:BLK, :]
        if at >= 2 * SIDE:
            test = test * weight_ref[0, 0]
        th, tl = split2(test)
        hi, lo = split2(mm(th, ch, NT) + (mm(th, cl, NT) + mm(tl, ch, NT)))
        prod_ref[at, 0:BLK, :] = hi
        prod_ref[at, BLK:, :] = lo
    near_kernel(targets, feat_ref, prod_ref, right_ref, *outs, *scratch)


def near_kernel(targets, feat_ref, prod_ref, right_ref, *refs):
    outs, (acc, buf_a, buf_b) = refs[:len(targets)], refs[len(targets):]
    acc[...] = jnp.zeros_like(acc)
    total = len(targets) * COUNT

    def left(t):
        return feat_ref[targets[0] + t // COUNT]

    def entries(t, buf):
        k = jnp.exp2(mm(left(t), right_ref[t % COUNT]))
        hi = k.astype(BF16)
        buf[:, BLK:] = hi
        buf[:, 0:BLK] = (k - hi.astype(F32)).astype(BF16)

    def fold(t, buf):
        b = t % COUNT
        acc[t // COUNT] += mm(buf[...], prod_ref[b]) + mm(buf[:, BLK:], prod_ref[b, 0:BLK, :])

    entries(0, buf_a)

    @pl.loop(0, total // 2)
    def _(u):
        t = 2 * u
        entries(t + 1, buf_b)
        fold(t, buf_a)
        entries(jnp.minimum(t + 2, total - 1), buf_a)
        fold(t + 1, buf_b)

    for i in range(len(targets)):
        outs[i][...] = acc[i]


def call(kernel, outs, n_smem, n_vmem, scratch=(), name=None, flops=0, trans=0):
    return pl.pallas_call(
        kernel,
        out_shape=[jax.ShapeDtypeStruct(s, t) for s, t in outs],
        in_specs=[pl.BlockSpec(memory_space=pltpu.SMEM)] * n_smem
        + [pl.BlockSpec(memory_space=VMEM)] * n_vmem,
        out_specs=[pl.BlockSpec(memory_space=VMEM)] * len(outs),
        scratch_shapes=list(scratch),
        compiler_params=pltpu.CompilerParams(vmem_limit_bytes=50 * 2**20),
        cost_estimate=pl.CostEstimate(flops=flops, bytes_accessed=4 * 2**20, transcendentals=trans),
        name=name,
    )


def near_scratch(targets):
    return [VMEM((len(targets), BLK, RANK), F32), VMEM((BLK, 2 * BLK), BF16), VMEM((BLK, 2 * BLK), BF16)]


SOLVE_SCRATCH = [VMEM((RANK, RANK), F32), VMEM((RANK, RANK), F32)]


def inverse_gram(picked, err_ref, inv_ref):
    gram = dot6(picked, picked, NT)
    eye = (
        lax.broadcasted_iota(jnp.int32, (RANK, RANK), 0)
        == lax.broadcasted_iota(jnp.int32, (RANK, RANK), 1)
    ).astype(F32)
    shift = jnp.sum(gram * eye) / RANK + 1e-06
    gram = gram + shift * eye
    bound = jnp.max(jnp.sum(jnp.abs(gram), axis=0, keepdims=True))
    alpha = 2.0 / (jnp.full((1, 1), 1.0, F32) * (bound + shift))
    err_ref[...] = eye - alpha * gram
    inv_ref[...] = alpha * eye

    def step(state):
        n, _ = state
        err = err_ref[...]
        eh, el = split2(err)
        ih, il = split2(inv_ref[...])
        inv_ref[...] += mm(ih, eh) + (mm(ih, el) + mm(il, eh))
        sq = mm(eh, eh) + (mm(eh, el) + mm(el, eh))
        err_ref[...] = sq
        return n + 1, jnp.sum(sq * sq)

    lax.while_loop(lambda st: (st[0] < 24) & (st[1] > 1e-6), step, (jnp.int32(0), jnp.float32(1e9)))

    def correct(state):
        inv = inv_ref[...]
        err = eye - dot6(gram, inv)
        inv_ref[...] = inv + dot3(inv, err)
        return state[0] + 1, jnp.sum(err * err)

    lax.while_loop(lambda st: (st[0] < 4) & (st[1] > 1e-5), correct, (jnp.int32(0), jnp.float32(1e9)))
    return inv_ref[...]


def solve_kernel(picked_ref, coeffs_ref, err_ref, inv_ref):
    picked = picked_ref[...]
    coeffs_ref[...] = dot3(inverse_gram(picked, err_ref, inv_ref), picked)


def basis_kernel(samp_ref, test_ref, coeffs_ref, *refs):
    parts, (basis_ref, proj_ref) = refs[:SIDE], refs[SIDE:]
    near_field = (parts[0][...] + parts[1][...]) + (parts[2][...] + parts[3][...])
    basis = dot3(samp_ref[...], coeffs_ref[...], NT) - near_field
    basis_ref[...] = basis
    proj_ref[...] = dot3(basis.T, test_ref[...])


def coupling(a, b):
    def norm3(v):
        return split3(v * v)

    ones = jnp.ones((RANK, DIM), BF16)
    inner = dot6(a, b, NT)
    na = sum(mm(p, ones, NT) for p in norm3(a))
    nb = sum(mm(ones, p, NT) for p in norm3(b))
    return jnp.exp2(-SCALE * (na + nb - 2.0 * inner))


EXT = SAMP + 2 * DIM
HALF = RANK // 2


def stack_node(lower, pick_own, skel_own, proj_own, pick_peer, skel_peer, proj_peer, stack_ref):
    def order(own, peer):
        return jnp.where(lower, own, peer), jnp.where(lower, peer, own)

    pick_a, pick_b = order(pick_own, pick_peer)
    proj_a, proj_b = order(proj_own, proj_peer)
    skel_a, skel_b = order(skel_own, skel_peer)
    stack_ref[0:RANK, :SAMP] = pick_a - dot3(coupling(skel_a[:, :DIM], skel_b[:, :DIM]), proj_b)
    stack_ref[RANK:, :SAMP] = pick_b - dot3(coupling(skel_b[:, :DIM], skel_a[:, :DIM]), proj_a)
    stack_ref[0:RANK, SAMP:] = skel_a
    stack_ref[RANK:, SAMP:] = skel_b


def picked_of(piv_ref, stack_ref):
    column = lax.broadcasted_iota(jnp.int32, (RANK, 2 * RANK), 1)
    one_hot = jnp.where(piv_ref[...] == column, 1.0, 0.0).astype(BF16)
    return pick(one_hot, stack_ref[...])


def half_of(lower, full):
    return jnp.where(lower, full[:HALF], full[HALF:])


def stack_kernel(
    info_ref, piv_ref, pick_own, skel_own, proj_own, pick_peer, skel_peer, proj_peer,
    stack_ref, picked_ref, skel_ref, send_ref
):
    lower = info_ref[0, 0] == 0
    stack_node(
        lower, pick_own[...], skel_own[...], proj_own[...],
        pick_peer[...], skel_peer[...], proj_peer[...], stack_ref,
    )
    picked = picked_of(piv_ref, stack_ref)
    picked_ref[...] = picked[:, :SAMP]
    skel_ref[...] = picked[:, SAMP:]
    send_ref[...] = half_of(lower, picked)


def mid_kernel(
    share, info_ref, stack_ref, picked_ref, proj_own, proj_peer, share_ref, proj_ref, send_ref, err_ref, inv_ref
):
    lower = info_ref[0, 0] == 0
    picked = picked_ref[...]
    coeffs = dot3(inverse_gram(picked, err_ref, inv_ref), picked)
    basis_t = dot3(coeffs, stack_ref[:, :SAMP], NT)
    left, right = basis_t[:, :RANK], basis_t[:, RANK:]
    proj = dot3(jnp.where(lower, left, right), proj_own[...]) + dot3(
        jnp.where(lower, right, left), proj_peer[...]
    )
    proj_ref[...] = proj
    send_ref[...] = half_of(lower, proj)
    rows = stack_ref[pl.ds(pl.multiple_of(info_ref[0, 1], 8), share), :SAMP]
    share_ref[...] = dot3(rows, coeffs, NT)


def top_kernel(
    share, info_ref, piv_ref, pick_own, skel_own, proj_own, pick_1, pick_2, proj_1, proj_2,
    share_ref, stack_ref, err_ref, inv_ref
):
    core0 = info_ref[0, 2] == 0

    def whole(first, second):
        f, o = first[...], second[...]
        return jnp.concatenate([jnp.where(core0, f, o), jnp.where(core0, o, f)], axis=0)

    peer = whole(pick_1, pick_2)
    stack_node(
        info_ref[0, 0] == 0, pick_own[...], skel_own[...], proj_own[...],
        peer[:, :SAMP], peer[:, SAMP:], whole(proj_1, proj_2), stack_ref,
    )
    picked = picked_of(piv_ref, stack_ref)[:, :SAMP]
    coeffs = dot3(inverse_gram(picked, err_ref, inv_ref), picked)
    rows = stack_ref[pl.ds(pl.multiple_of(info_ref[0, 1], 8), share), :SAMP]
    share_ref[...] = dot3(rows, coeffs, NT)


def after(first, *then):
    return lax.optimization_barrier((first, *then))


def sum_row(part, *then):
    share = part.shape[0] // 16
    parts = lax.all_to_all(part.reshape(16, share, -1), "row", 0, 0)
    mine, *then = after(jnp.sum(parts, axis=0), *then)
    every = lax.all_to_all(jnp.broadcast_to(mine[None], (16, *mine.shape)), "row", 0, 0)
    return (every.reshape(part.shape), *then)


def body(points, samples, test_matrix, near_mask, leaf_pivots, mid_pivots, top_pivots):
    leaf = lax.axis_index("leaf")
    row = lax.axis_index("row")
    core = leaf & 1
    start = (row * BLK).reshape(1, 1)
    xt = points.T
    pivots = leaf_pivots[0].reshape(RANK, 1)
    weight = jnp.where(core == 0, near_mask[0, 0], near_mask[0, 1]).astype(F32).reshape(1, 1)

    (skel,) = call(skel_kernel, [((RANK, 2 * DIM), F32)], 1, 2, name="skel")(start, pivots, xt)
    skel, message, xt = after(skel, jnp.concatenate([test_matrix, xt], axis=0), xt)
    own = [message, lax.ppermute(message, "row", along_x(1)), lax.ppermute(message, "row", along_x(3))]
    sib = [lax.ppermute(message, "leaf", SIBLING)]
    outer = [lax.ppermute(message, "leaf", OUTER)]
    skel, message = sum_row(skel, message)
    own.append(lax.ppermute(message, "row", along_x(2)))
    (part,) = call(
        pivot_kernel, [((RANK, SAMP), F32)], 2, 6, [VMEM((4 * DIM, BLK), BF16)], name="pivot", flops=2 * 10**9
    )(start, weight, pivots, skel, samples, own[0], sib[0], outer[0])
    part, xt, own[1], own[2] = after(part, xt, own[1], own[2])
    (feats,) = call(feature_kernel, [((SIDE, BLK, 4 * DIM), BF16)], 0, 4, name="features")(
        xt, *[lax.ppermute(xt, "row", along_y(k)) for k in SHIFTS]
    )
    picked, own[3] = sum_row(part, own[3])
    sib += [lax.ppermute(m, "leaf", SIBLING) for m in own[1:]]
    outer += [lax.ppermute(m, "leaf", OUTER) for m in own[1:]]
    (coeffs,) = call(
        solve_kernel, [((RANK, SAMP), F32)], 0, 1, SOLVE_SCRATCH, name="solve", flops=3 * 10**9
    )(picked)
    picked_sib = lax.ppermute(picked, "leaf", SIBLING)
    skel_sib = lax.ppermute(skel, "leaf", SIBLING)

    block = ((BLK, RANK), F32)
    sum_1, sum_3, sum_2, prods, rights = call(
        functools.partial(far_kernel, (1, 2, 3)),
        [block] * 3 + [((COUNT, 2 * BLK, RANK), BF16), ((COUNT, 4 * DIM, BLK), BF16)], 1, 2 + COUNT,
        near_scratch((1, 2, 3)), name="near_far", flops=30 * 10**9,
    )(weight, coeffs, feats, *own, *sib, *outer)
    sum_2 = lax.ppermute(sum_2, "row", along_y(-2))
    sum_1 = lax.ppermute(sum_1, "row", along_y(-1))
    sum_3 = lax.ppermute(sum_3, "row", along_y(-3))
    (sum_0,) = call(
        functools.partial(near_kernel, (0,)), [block], 0, 3, near_scratch((0,)), name="near_own", flops=10**9
    )(feats, prods, rights)
    leaf_basis, proj = call(
        basis_kernel, [block, ((RANK, SAMP), F32)], 0, 3 + SIDE, name="basis", flops=10**9
    )(samples, test_matrix, coeffs, sum_0, sum_1, sum_2, sum_3)
    (proj,) = sum_row(proj)
    proj_sib = lax.ppermute(proj, "leaf", SIBLING)

    def info(lower, first):
        return jnp.stack([lower, first, core]).astype(jnp.int32).reshape(1, 3)

    def row_of(table, node):
        return lax.dynamic_index_in_dim(table, node, 0, keepdims=False).reshape(RANK, 1)

    node = ((RANK, SAMP), F32)
    mid_share, top_share = RANK // 16, RANK // 32
    mid_info = info(core, core * RANK + row * mid_share)
    stack, picked, skel, send = call(
        stack_kernel, [((2 * RANK, EXT), F32), node, ((RANK, 2 * DIM), F32), ((HALF, EXT), F32)], 1, 7,
        name="mid_stack", flops=10**9,
    )(mid_info, row_of(mid_pivots, leaf >> 1), picked, skel, proj, picked_sib, skel_sib, proj_sib)
    pick_1 = lax.ppermute(send, "leaf", COUSIN)
    pick_2 = lax.ppermute(pick_1, "leaf", SIBLING)
    mid_basis, proj, send = call(
        functools.partial(mid_kernel, mid_share),
        [((mid_share, RANK), F32), node, ((HALF, SAMP), F32)], 1, 4, SOLVE_SCRATCH,
        name="mid_solve", flops=3 * 10**9,
    )(mid_info, stack, picked, proj, proj_sib)
    proj_1 = lax.ppermute(send, "leaf", COUSIN)
    proj_2 = lax.ppermute(proj_1, "leaf", SIBLING)
    second = leaf >> 1 & 1
    (top_basis,) = call(
        functools.partial(top_kernel, top_share), [((top_share, RANK), F32)], 1, 8,
        [VMEM((2 * RANK, EXT), F32), *SOLVE_SCRATCH], name="top", flops=3 * 10**9,
    )(
        info(second, second * RANK + core * (RANK // 2) + row * top_share), row_of(top_pivots, leaf >> 2),
        picked, skel, proj, pick_1, pick_2, proj_1, proj_2,
    )
    return (leaf_basis, mid_basis, top_basis)


def solution(mesh):
    split = P(("leaf", "row"), None)
    return jax.shard_map(
        body,
        mesh=mesh,
        in_specs=(split, split, split, P("leaf", None), P("leaf", None), P(), P()),
        out_specs=(split, split, split),
        check_vma=False,
    )
```

```python
import functools
import math

import jax
import jax.numpy as jnp
from jax import lax
from jax.experimental import pallas as pl
from jax.experimental.pallas import tpu as pltpu
from jax.sharding import PartitionSpec as P

DIM = 64
RANK = 256
SAMP = 512
BLK = 512
SIDE = 4
SCALE = math.log2(math.e) / DIM
HIGHEST = lax.Precision.HIGHEST
F32, BF16 = jnp.float32, jnp.bfloat16
VMEM = pltpu.VMEM


def shift(dx, dy):
    return [(4 * x + y, 4 * ((x + dx) % 4) + (y + dy) % 4) for x in range(4) for y in range(4)]


SIBLING = [(i, i ^ 1) for i in range(8)]
OUTER = [(1, 2), (2, 1), (3, 4), (4, 3), (5, 6), (6, 5)]
COUSIN = [(i, i ^ 2) for i in range(8)]


NN = (((1,), (0,)), ((), ()))
NT = (((1,), (1,)), ((), ()))


def mm(a, b, dims=NN):
    return lax.dot_general(a, b, dims, preferred_element_type=F32)


def split2(a):
    hi = a.astype(BF16)
    return hi, (a - hi.astype(F32)).astype(BF16)


def split3(a):
    hi = a.astype(BF16)
    rest = a - hi.astype(F32)
    mid = rest.astype(BF16)
    return hi, mid, (rest - mid.astype(F32)).astype(BF16)


def dot3(a, b, dims=NN):
    ah, al = split2(a)
    bh, bl = split2(b)
    return mm(ah, bh, dims) + (mm(ah, bl, dims) + mm(al, bh, dims))


def dot6(a, b, dims=NN):
    ah, am, al = split3(a)
    bh, bm, bl = split3(b)
    return mm(ah, bh, dims) + (
        (mm(ah, bm, dims) + mm(am, bh, dims))
        + (mm(am, bm, dims) + (mm(ah, bl, dims) + mm(al, bh, dims)))
    )


def pick(one_hot, a):
    h, m, l = split3(a)
    return (mm(one_hot, h) + mm(one_hot, m)) + mm(one_hot, l)


SOURCE = ((-1, 0), (0, -1), (1, 1))
TARGET = ((2, 0), (0, 2), (2, 2))
COUNT = 3 * SIDE


def norm_rows(xt, first):
    rows = lax.broadcasted_iota(jnp.int32, (DIM, BLK), 0)
    sq = jnp.sum(xt * xt, axis=0, keepdims=True) * (-SCALE)
    h, m, l = (v.astype(F32) for v in split3(sq))
    one = jnp.ones_like(sq)
    aux = jnp.zeros((DIM, BLK), F32)
    for n, part in enumerate((h, m, l, one, one, one) if first else (one, one, one, h, m, l)):
        aux = jnp.where(rows == n, part, aux)
    return aux


def left_features(xt):
    scaled = xt * (2.0 * SCALE)
    hi = scaled.astype(BF16).astype(F32)
    feat = jnp.concatenate([hi, hi, scaled - hi, norm_rows(xt, True)], axis=0)
    return feat.T.astype(BF16)


def right_features(xt, ref):
    hi, lo = split2(xt)
    ref[0:DIM, :] = hi
    ref[DIM:2 * DIM, :] = lo
    ref[2 * DIM:3 * DIM, :] = hi
    ref[3 * DIM:, :] = norm_rows(xt, False).astype(BF16)


def rows_of(start, piv_ref):
    column = lax.broadcasted_iota(jnp.int32, (RANK, BLK), 1)
    return jnp.where(piv_ref[...] == column + start, 1.0, 0.0).astype(BF16)


def skel_kernel(start_ref, piv_ref, points_ref, skel_ref):
    one_hot = rows_of(start_ref[0, 0], piv_ref)
    skel = sum(mm(one_hot, part, NT) for part in split3(points_ref[...]))
    skel_ref[...] = jnp.concatenate([skel, jnp.zeros((RANK, DIM), F32)], axis=1)


def feature_kernel(p0, p1, p2, p3, feat_ref):
    for i, ref in enumerate((p0, p1, p2, p3)):
        feat_ref[i] = left_features(ref[...])


def pivot_kernel(
    start_ref, weight_ref, piv_ref, skel_ref, samp_ref, own_ref, sib_ref, out_ref, part_ref, right_ref
):
    skel = skel_ref[:, :DIM]
    scaled = skel * (2.0 * SCALE)
    hi = scaled.astype(BF16).astype(F32)
    lane = lax.broadcasted_iota(jnp.int32, (RANK, DIM), 1)
    sq = jnp.sum(skel * skel, axis=1, keepdims=True) * (-SCALE)
    aux = jnp.where(lane < 6, 1.0, 0.0)
    for n, part in enumerate(split3(sq)):
        aux = jnp.where(lane == n, part.astype(F32), aux)
    feat = jnp.concatenate([hi, hi, scaled - hi, aux], axis=1).astype(BF16)
    total = pick(rows_of(start_ref[0, 0], piv_ref), samp_ref[...])
    for n, ref in enumerate((own_ref, sib_ref, out_ref)):
        right_features(ref[BLK:, :], right_ref)
        kern = jnp.exp2(mm(feat, right_ref[...]))
        if n == 2:
            kern = kern * weight_ref[0, 0]
        total -= dot3(kern, ref[0:BLK, :])
    part_ref[...] = total


def far_kernel(targets, weight_ref, coeffs_ref, feat_ref, *refs):
    msgs, refs = refs[:COUNT], refs[COUNT:]
    outs, (prod_ref, right_ref), scratch = refs[:len(targets)], refs[len(targets):-3], refs[-3:]
    ch, cl = split2(coeffs_ref[...])
    for at, ref in enumerate(msgs):
        right_features(ref[BLK:, :], right_ref.at[at])
        test = ref[0:BLK, :]
        if at >= 2 * SIDE:
            test = test * weight_ref[0, 0]
        th, tl = split2(test)
        hi, lo = split2(mm(th, ch, NT) + (mm(th, cl, NT) + mm(tl, ch, NT)))
        prod_ref[at, 0:BLK, :] = hi
        prod_ref[at, BLK:, :] = lo
    near_kernel(targets, feat_ref, prod_ref, right_ref, *outs, *scratch)


def near_kernel(targets, feat_ref, prod_ref, right_ref, *refs):
    before, outs, (acc, buf_a, buf_b) = refs[:-3 - len(targets)], refs[-3 - len(targets):-3], refs[-3:]
    acc[...] = jnp.zeros_like(acc)
    for ref in before:
        acc[0] += ref[...]
    total = len(targets) * COUNT

    def left(t):
        return feat_ref[targets[0] + t // COUNT]

    def entries(t, buf):
        k = jnp.exp2(mm(left(t), right_ref[t % COUNT]))
        hi = k.astype(BF16)
        buf[:, BLK:] = hi
        buf[:, 0:BLK] = (k - hi.astype(F32)).astype(BF16)

    def fold(t, buf):
        b = t % COUNT
        acc[t // COUNT] += mm(buf[...], prod_ref[b]) + mm(buf[:, BLK:], prod_ref[b, 0:BLK, :])

    entries(0, buf_a)

    @pl.loop(0, total // 2)
    def _(u):
        t = 2 * u
        entries(t + 1, buf_b)
        fold(t, buf_a)
        entries(jnp.minimum(t + 2, total - 1), buf_a)
        fold(t + 1, buf_b)

    for i in range(len(targets)):
        outs[i][...] = acc[i]


def call(kernel, outs, n_smem, n_vmem, scratch=(), name=None, flops=0, trans=0):
    return pl.pallas_call(
        kernel,
        out_shape=[jax.ShapeDtypeStruct(s, t) for s, t in outs],
        in_specs=[pl.BlockSpec(memory_space=pltpu.SMEM)] * n_smem
        + [pl.BlockSpec(memory_space=VMEM)] * n_vmem,
        out_specs=[pl.BlockSpec(memory_space=VMEM)] * len(outs),
        scratch_shapes=list(scratch),
        compiler_params=pltpu.CompilerParams(vmem_limit_bytes=50 * 2**20),
        cost_estimate=pl.CostEstimate(flops=flops, bytes_accessed=4 * 2**20, transcendentals=trans),
        name=name,
    )


def near_scratch(targets):
    return [VMEM((len(targets), BLK, RANK), F32), VMEM((BLK, 2 * BLK), BF16), VMEM((BLK, 2 * BLK), BF16)]


SOLVE_SCRATCH = [VMEM((RANK, RANK), F32), VMEM((RANK, RANK), F32)]


def inverse_gram(picked, err_ref, inv_ref):
    gram = dot6(picked, picked, NT)
    eye = (
        lax.broadcasted_iota(jnp.int32, (RANK, RANK), 0)
        == lax.broadcasted_iota(jnp.int32, (RANK, RANK), 1)
    ).astype(F32)
    shift = jnp.sum(gram * eye) / RANK + 1e-06
    gram = gram + shift * eye
    bound = jnp.max(jnp.sum(jnp.abs(gram), axis=0, keepdims=True))
    alpha = 2.0 / (jnp.full((1, 1), 1.0, F32) * (bound + shift))
    err_ref[...] = eye - alpha * gram
    inv_ref[...] = alpha * eye

    def step(state):
        n, _ = state
        err = err_ref[...]
        eh, el = split2(err)
        ih, il = split2(inv_ref[...])
        inv_ref[...] += mm(ih, eh) + (mm(ih, el) + mm(il, eh))
        sq = mm(eh, eh) + (mm(eh, el) + mm(el, eh))
        err_ref[...] = sq
        return n + 1, jnp.sum(sq * sq)

    lax.while_loop(lambda st: (st[0] < 24) & (st[1] > 1e-6), step, (jnp.int32(0), jnp.float32(1e9)))

    def correct(state):
        inv = inv_ref[...]
        err = eye - dot6(gram, inv)
        inv_ref[...] = inv + dot3(inv, err)
        return state[0] + 1, jnp.sum(err * err)

    lax.while_loop(lambda st: (st[0] < 4) & (st[1] > 1e-5), correct, (jnp.int32(0), jnp.float32(1e9)))
    return inv_ref[...]


def solve_kernel(picked_ref, coeffs_ref, err_ref, inv_ref):
    picked = picked_ref[...]
    coeffs_ref[...] = dot3(inverse_gram(picked, err_ref, inv_ref), picked)


def basis_kernel(samp_ref, test_ref, coeffs_ref, *refs):
    parts, (basis_ref, proj_ref) = refs[:3], refs[3:]
    near_field = parts[0][...] + (parts[1][...] + parts[2][...])
    basis = dot3(samp_ref[...], coeffs_ref[...], NT) - near_field
    basis_ref[...] = basis
    proj_ref[...] = dot3(basis.T, test_ref[...])


def coupling(a, b):
    def norm3(v):
        return split3(v * v)

    ones = jnp.ones((RANK, DIM), BF16)
    inner = dot6(a, b, NT)
    na = sum(mm(p, ones, NT) for p in norm3(a))
    nb = sum(mm(ones, p, NT) for p in norm3(b))
    return jnp.exp2(-SCALE * (na + nb - 2.0 * inner))


EXT = SAMP + 2 * DIM
HALF = RANK // 2


def stack_node(lower, pick_own, skel_own, proj_own, pick_peer, skel_peer, proj_peer, stack_ref):
    def order(own, peer):
        return jnp.where(lower, own, peer), jnp.where(lower, peer, own)

    pick_a, pick_b = order(pick_own, pick_peer)
    proj_a, proj_b = order(proj_own, proj_peer)
    skel_a, skel_b = order(skel_own, skel_peer)
    stack_ref[0:RANK, :SAMP] = pick_a - dot3(coupling(skel_a[:, :DIM], skel_b[:, :DIM]), proj_b)
    stack_ref[RANK:, :SAMP] = pick_b - dot3(coupling(skel_b[:, :DIM], skel_a[:, :DIM]), proj_a)
    stack_ref[0:RANK, SAMP:] = skel_a
    stack_ref[RANK:, SAMP:] = skel_b


def picked_of(piv_ref, stack_ref):
    column = lax.broadcasted_iota(jnp.int32, (RANK, 2 * RANK), 1)
    one_hot = jnp.where(piv_ref[...] == column, 1.0, 0.0).astype(BF16)
    return pick(one_hot, stack_ref[...])


def half_of(lower, full):
    return jnp.where(lower, full[:HALF], full[HALF:])


def stack_kernel(
    info_ref, piv_ref, pick_own, skel_own, proj_own, pick_peer, skel_peer, proj_peer,
    stack_ref, picked_ref, skel_ref, send_ref
):
    lower = info_ref[0, 0] == 0
    stack_node(
        lower, pick_own[...], skel_own[...], proj_own[...],
        pick_peer[...], skel_peer[...], proj_peer[...], stack_ref,
    )
    picked = picked_of(piv_ref, stack_ref)
    picked_ref[...] = picked[:, :SAMP]
    skel_ref[...] = picked[:, SAMP:]
    send_ref[...] = half_of(lower, picked)


def mid_kernel(
    share, info_ref, stack_ref, picked_ref, proj_own, proj_peer, share_ref, proj_ref, send_ref, err_ref, inv_ref
):
    lower = info_ref[0, 0] == 0
    picked = picked_ref[...]
    coeffs = dot3(inverse_gram(picked, err_ref, inv_ref), picked)
    basis_t = dot3(coeffs, stack_ref[:, :SAMP], NT)
    left, right = basis_t[:, :RANK], basis_t[:, RANK:]
    proj = dot3(jnp.where(lower, left, right), proj_own[...]) + dot3(
        jnp.where(lower, right, left), proj_peer[...]
    )
    proj_ref[...] = proj
    send_ref[...] = half_of(lower, proj)
    rows = stack_ref[pl.ds(pl.multiple_of(info_ref[0, 1], 8), share), :SAMP]
    share_ref[...] = dot3(rows, coeffs, NT)


def top_kernel(
    share, info_ref, piv_ref, pick_own, skel_own, proj_own, pick_1, pick_2, proj_1, proj_2,
    share_ref, stack_ref, err_ref, inv_ref
):
    core0 = info_ref[0, 2] == 0

    def whole(first, second):
        f, o = first[...], second[...]
        return jnp.concatenate([jnp.where(core0, f, o), jnp.where(core0, o, f)], axis=0)

    peer = whole(pick_1, pick_2)
    stack_node(
        info_ref[0, 0] == 0, pick_own[...], skel_own[...], proj_own[...],
        peer[:, :SAMP], peer[:, SAMP:], whole(proj_1, proj_2), stack_ref,
    )
    picked = picked_of(piv_ref, stack_ref)[:, :SAMP]
    coeffs = dot3(inverse_gram(picked, err_ref, inv_ref), picked)
    rows = stack_ref[pl.ds(pl.multiple_of(info_ref[0, 1], 8), share), :SAMP]
    share_ref[...] = dot3(rows, coeffs, NT)


def after(first, *then):
    return lax.optimization_barrier((first, *then))


def sum_row(part, *then):
    share = part.shape[0] // 16
    parts = lax.all_to_all(part.reshape(16, share, -1), "row", 0, 0)
    mine, *then = after(jnp.sum(parts, axis=0), *then)
    every = lax.all_to_all(jnp.broadcast_to(mine[None], (16, *mine.shape)), "row", 0, 0)
    return (every.reshape(part.shape), *then)


def body(points, samples, test_matrix, near_mask, leaf_pivots, mid_pivots, top_pivots):
    leaf = lax.axis_index("leaf")
    row = lax.axis_index("row")
    core = leaf & 1
    start = (row * BLK).reshape(1, 1)
    xt = points.T
    pivots = leaf_pivots[0].reshape(RANK, 1)
    weight = jnp.where(core == 0, near_mask[0, 0], near_mask[0, 1]).astype(F32).reshape(1, 1)

    (skel,) = call(skel_kernel, [((RANK, 2 * DIM), F32)], 1, 2, name="skel")(start, pivots, xt)
    skel, message = after(skel, jnp.concatenate([test_matrix, xt], axis=0))
    own = [message]
    sib = [lax.ppermute(message, "leaf", SIBLING)]
    outer = [lax.ppermute(message, "leaf", OUTER)]
    skel, message = sum_row(skel, message)
    own += [lax.ppermute(message, "row", shift(*by)) for by in SOURCE]
    (part,) = call(
        pivot_kernel, [((RANK, SAMP), F32)], 2, 6, [VMEM((4 * DIM, BLK), BF16)], name="pivot", flops=2 * 10**9
    )(start, weight, pivots, skel, samples, own[0], sib[0], outer[0])
    part, *own[1:] = after(part, *own[1:])
    sib += [lax.ppermute(m, "leaf", SIBLING) for m in own[1:]]
    outer += [lax.ppermute(m, "leaf", OUTER) for m in own[1:]]
    picked, xt = sum_row(part, xt)
    (feats,) = call(feature_kernel, [((SIDE, BLK, 4 * DIM), BF16)], 0, 4, name="features")(
        xt, *[lax.ppermute(xt, "row", shift(*by)) for by in TARGET]
    )
    (coeffs,) = call(
        solve_kernel, [((RANK, SAMP), F32)], 0, 1, SOLVE_SCRATCH, name="solve", flops=3 * 10**9
    )(picked)
    picked_sib = lax.ppermute(picked, "leaf", SIBLING)
    skel_sib = lax.ppermute(skel, "leaf", SIBLING)

    block = ((BLK, RANK), F32)
    sum_3, prods, rights = call(
        functools.partial(far_kernel, (3,)),
        [block] + [((COUNT, 2 * BLK, RANK), BF16), ((COUNT, 4 * DIM, BLK), BF16)], 1, 2 + COUNT,
        near_scratch((3,)), name="near_3", flops=10**10,
    )(weight, coeffs, feats, *own, *sib, *outer)
    got_3 = lax.ppermute(sum_3, "row", shift(*TARGET[2]))
    sum_1, sum_2 = call(
        functools.partial(near_kernel, (1, 2)), [block] * 2, 0, 3, near_scratch((1, 2)), name="near_12", flops=2 * 10**10,
    )(feats, prods, rights)
    got_1 = lax.ppermute(sum_1, "row", shift(*TARGET[0]))
    got_2 = lax.ppermute(sum_2, "row", shift(*TARGET[1]))
    (sum_0,) = call(
        functools.partial(near_kernel, (0,)), [block], 0, 4, near_scratch((0,)), name="near_0", flops=10**10
    )(feats, prods, rights, got_3)
    leaf_basis, proj = call(
        basis_kernel, [block, ((RANK, SAMP), F32)], 0, 6, name="basis", flops=10**9
    )(samples, test_matrix, coeffs, sum_0, got_1, got_2)
    (proj,) = sum_row(proj)
    proj_sib = lax.ppermute(proj, "leaf", SIBLING)

    def info(lower, first):
        return jnp.stack([lower, first, core]).astype(jnp.int32).reshape(1, 3)

    def row_of(table, node):
        return lax.dynamic_index_in_dim(table, node, 0, keepdims=False).reshape(RANK, 1)

    node = ((RANK, SAMP), F32)
    mid_share, top_share = RANK // 16, RANK // 32
    mid_info = info(core, core * RANK + row * mid_share)
    stack, picked, skel, send = call(
        stack_kernel, [((2 * RANK, EXT), F32), node, ((RANK, 2 * DIM), F32), ((HALF, EXT), F32)], 1, 7,
        name="mid_stack", flops=10**9,
    )(mid_info, row_of(mid_pivots, leaf >> 1), picked, skel, proj, picked_sib, skel_sib, proj_sib)
    pick_1 = lax.ppermute(send, "leaf", COUSIN)
    pick_2 = lax.ppermute(pick_1, "leaf", SIBLING)
    mid_basis, proj, send = call(
        functools.partial(mid_kernel, mid_share),
        [((mid_share, RANK), F32), node, ((HALF, SAMP), F32)], 1, 4, SOLVE_SCRATCH,
        name="mid_solve", flops=3 * 10**9,
    )(mid_info, stack, picked, proj, proj_sib)
    proj_1 = lax.ppermute(send, "leaf", COUSIN)
    proj_2 = lax.ppermute(proj_1, "leaf", SIBLING)
    second = leaf >> 1 & 1
    (top_basis,) = call(
        functools.partial(top_kernel, top_share), [((top_share, RANK), F32)], 1, 8,
        [VMEM((2 * RANK, EXT), F32), *SOLVE_SCRATCH], name="top", flops=3 * 10**9,
    )(
        info(second, second * RANK + core * (RANK // 2) + row * top_share), row_of(top_pivots, leaf >> 2),
        picked, skel, proj, pick_1, pick_2, proj_1, proj_2,
    )
    return (leaf_basis, mid_basis, top_basis)


def solution(mesh):
    split = P(("leaf", "row"), None)
    return jax.shard_map(
        body,
        mesh=mesh,
        in_specs=(split, split, split, P("leaf", None), P("leaf", None), P(), P()),
        out_specs=(split, split, split),
        check_vma=False,
    )
```

```python
import functools
import math

import jax
import jax.numpy as jnp
from jax import lax
from jax.experimental import pallas as pl
from jax.experimental.pallas import tpu as pltpu
from jax.sharding import PartitionSpec as P

DIM = 64
RANK = 256
SAMP = 512
BLK = 512
SIDE = 4
SCALE = math.log2(math.e) / DIM
HIGHEST = lax.Precision.HIGHEST
F32, BF16 = jnp.float32, jnp.bfloat16
VMEM = pltpu.VMEM


def shift(dx, dy):
    return [(4 * x + y, 4 * ((x + dx) % 4) + (y + dy) % 4) for x in range(4) for y in range(4)]


SIBLING = [(i, i ^ 1) for i in range(8)]
OUTER = [(1, 2), (2, 1), (3, 4), (4, 3), (5, 6), (6, 5)]
COUSIN = [(i, i ^ 2) for i in range(8)]


NN = (((1,), (0,)), ((), ()))
NT = (((1,), (1,)), ((), ()))


def mm(a, b, dims=NN):
    return lax.dot_general(a, b, dims, preferred_element_type=F32)


def split2(a):
    hi = a.astype(BF16)
    return hi, (a - hi.astype(F32)).astype(BF16)


def split3(a):
    hi = a.astype(BF16)
    rest = a - hi.astype(F32)
    mid = rest.astype(BF16)
    return hi, mid, (rest - mid.astype(F32)).astype(BF16)


def dot3(a, b, dims=NN):
    ah, al = split2(a)
    bh, bl = split2(b)
    return mm(ah, bh, dims) + (mm(ah, bl, dims) + mm(al, bh, dims))


def dot6(a, b, dims=NN):
    ah, am, al = split3(a)
    bh, bm, bl = split3(b)
    return mm(ah, bh, dims) + (
        (mm(ah, bm, dims) + mm(am, bh, dims))
        + (mm(am, bm, dims) + (mm(ah, bl, dims) + mm(al, bh, dims)))
    )


def pick(one_hot, a):
    h, m, l = split3(a)
    return (mm(one_hot, h) + mm(one_hot, m)) + mm(one_hot, l)


SOURCE = ((-1, 0), (0, -1), (1, 1))
TARGET = ((2, 0), (0, 2), (2, 2))
COUNT = 3 * SIDE


def norm_rows(xt, first):
    rows = lax.broadcasted_iota(jnp.int32, (DIM, BLK), 0)
    sq = jnp.sum(xt * xt, axis=0, keepdims=True) * (-SCALE)
    h, m, l = (v.astype(F32) for v in split3(sq))
    one = jnp.ones_like(sq)
    aux = jnp.zeros((DIM, BLK), F32)
    for n, part in enumerate((h, m, l, one, one, one) if first else (one, one, one, h, m, l)):
        aux = jnp.where(rows == n, part, aux)
    return aux


def left_features(xt):
    scaled = xt * (2.0 * SCALE)
    hi = scaled.astype(BF16).astype(F32)
    feat = jnp.concatenate([hi, hi, scaled - hi, norm_rows(xt, True)], axis=0)
    return feat.T.astype(BF16)


def right_features(xt, ref):
    hi, lo = split2(xt)
    ref[0:DIM, :] = hi
    ref[DIM:2 * DIM, :] = lo
    ref[2 * DIM:3 * DIM, :] = hi
    ref[3 * DIM:, :] = norm_rows(xt, False).astype(BF16)


def rows_of(start, piv_ref):
    column = lax.broadcasted_iota(jnp.int32, (RANK, BLK), 1)
    return jnp.where(piv_ref[...] == column + start, 1.0, 0.0).astype(BF16)


def skel_kernel(start_ref, piv_ref, points_ref, skel_ref):
    one_hot = rows_of(start_ref[0, 0], piv_ref)
    skel = sum(mm(one_hot, part, NT) for part in split3(points_ref[...]))
    skel_ref[...] = jnp.concatenate([skel, jnp.zeros((RANK, DIM), F32)], axis=1)


def feature_kernel(p0, p1, p2, p3, feat_ref):
    for i, ref in enumerate((p0, p1, p2, p3)):
        feat_ref[i] = left_features(ref[...])


def pivot_kernel(
    start_ref, weight_ref, piv_ref, skel_ref, samp_ref, own_ref, sib_ref, out_ref, part_ref, right_ref
):
    skel = skel_ref[:, :DIM]
    scaled = skel * (2.0 * SCALE)
    hi = scaled.astype(BF16).astype(F32)
    lane = lax.broadcasted_iota(jnp.int32, (RANK, DIM), 1)
    sq = jnp.sum(skel * skel, axis=1, keepdims=True) * (-SCALE)
    aux = jnp.where(lane < 6, 1.0, 0.0)
    for n, part in enumerate(split3(sq)):
        aux = jnp.where(lane == n, part.astype(F32), aux)
    feat = jnp.concatenate([hi, hi, scaled - hi, aux], axis=1).astype(BF16)
    total = pick(rows_of(start_ref[0, 0], piv_ref), samp_ref[...])
    for n, ref in enumerate((own_ref, sib_ref, out_ref)):
        right_features(ref[BLK:, :], right_ref)
        kern = jnp.exp2(mm(feat, right_ref[...]))
        if n == 2:
            kern = kern * weight_ref[0, 0]
        total -= dot3(kern, ref[0:BLK, :])
    part_ref[...] = total


def far_kernel(targets, weight_ref, coeffs_ref, feat_ref, *refs):
    msgs, refs = refs[:6], refs[6:]
    outs, (prod_ref, right_ref), scratch = refs[:len(targets)], refs[len(targets):-3], refs[-3:]
    ch, cl = split2(coeffs_ref[...])
    for at in range(COUNT):
        n, place = divmod(at, SIDE)
        ref, first = (msgs[2 * n + 1], (place - 1) * (BLK + DIM)) if place else (msgs[2 * n], 0)
        right_features(ref[first + BLK:first + BLK + DIM, :], right_ref.at[at])
        test = ref[first:first + BLK, :]
        if at >= 2 * SIDE:
            test = test * weight_ref[0, 0]
        th, tl = split2(test)
        hi, lo = split2(mm(th, ch, NT) + (mm(th, cl, NT) + mm(tl, ch, NT)))
        prod_ref[at, 0:BLK, :] = hi
        prod_ref[at, BLK:, :] = lo
    near_kernel(targets, feat_ref, prod_ref, right_ref, *outs, *scratch)


def near_kernel(targets, feat_ref, prod_ref, right_ref, *refs):
    before, outs, (acc, buf_a, buf_b) = refs[:-3 - len(targets)], refs[-3 - len(targets):-3], refs[-3:]
    acc[...] = jnp.zeros_like(acc)
    for ref in before:
        acc[0] += ref[...]
    total = len(targets) * COUNT

    def left(t):
        return feat_ref[targets[0] + t // COUNT]

    def entries(t, buf):
        k = jnp.exp2(mm(left(t), right_ref[t % COUNT]))
        hi = k.astype(BF16)
        buf[:, BLK:] = hi
        buf[:, 0:BLK] = (k - hi.astype(F32)).astype(BF16)

    def fold(t, buf):
        b = t % COUNT
        acc[t // COUNT] += mm(buf[...], prod_ref[b]) + mm(buf[:, BLK:], prod_ref[b, 0:BLK, :])

    entries(0, buf_a)

    @pl.loop(0, total // 2)
    def _(u):
        t = 2 * u
        entries(t + 1, buf_b)
        fold(t, buf_a)
        entries(jnp.minimum(t + 2, total - 1), buf_a)
        fold(t + 1, buf_b)

    for i in range(len(targets)):
        outs[i][...] = acc[i]


def call(kernel, outs, n_smem, n_vmem, scratch=(), name=None, flops=0, trans=0):
    return pl.pallas_call(
        kernel,
        out_shape=[jax.ShapeDtypeStruct(s, t) for s, t in outs],
        in_specs=[pl.BlockSpec(memory_space=pltpu.SMEM)] * n_smem
        + [pl.BlockSpec(memory_space=VMEM)] * n_vmem,
        out_specs=[pl.BlockSpec(memory_space=VMEM)] * len(outs),
        scratch_shapes=list(scratch),
        compiler_params=pltpu.CompilerParams(vmem_limit_bytes=50 * 2**20),
        cost_estimate=pl.CostEstimate(flops=flops, bytes_accessed=2**16, transcendentals=trans),
        name=name,
    )


def near_scratch(targets):
    return [VMEM((len(targets), BLK, RANK), F32), VMEM((BLK, 2 * BLK), BF16), VMEM((BLK, 2 * BLK), BF16)]


SOLVE_SCRATCH = [VMEM((RANK, RANK), F32), VMEM((RANK, RANK), F32)]


def inverse_gram(picked, err_ref, inv_ref):
    gram = dot6(picked, picked, NT)
    eye = (
        lax.broadcasted_iota(jnp.int32, (RANK, RANK), 0)
        == lax.broadcasted_iota(jnp.int32, (RANK, RANK), 1)
    ).astype(F32)
    shift = jnp.sum(gram * eye) / RANK + 1e-06
    gram = gram + shift * eye
    bound = jnp.max(jnp.sum(jnp.abs(gram), axis=0, keepdims=True))
    alpha = 2.0 / (jnp.full((1, 1), 1.0, F32) * (bound + shift))
    err_ref[...] = eye - alpha * gram
    inv_ref[...] = alpha * eye

    def step(state):
        n, _ = state
        err = err_ref[...]
        eh, el = split2(err)
        ih, il = split2(inv_ref[...])
        inv_ref[...] += mm(ih, eh) + (mm(ih, el) + mm(il, eh))
        sq = mm(eh, eh) + (mm(eh, el) + mm(el, eh))
        err_ref[...] = sq
        return n + 1, jnp.sum(sq * sq)

    lax.while_loop(lambda st: (st[0] < 24) & (st[1] > 1e-6), step, (jnp.int32(0), jnp.float32(1e9)))

    def correct(state):
        inv = inv_ref[...]
        err = eye - dot6(gram, inv)
        inv_ref[...] = inv + dot3(inv, err)
        return state[0] + 1, jnp.sum(err * err)

    lax.while_loop(lambda st: (st[0] < 4) & (st[1] > 1e-5), correct, (jnp.int32(0), jnp.float32(1e9)))
    return inv_ref[...]


def solve_kernel(picked_ref, coeffs_ref, err_ref, inv_ref):
    picked = picked_ref[...]
    coeffs_ref[...] = dot3(inverse_gram(picked, err_ref, inv_ref), picked)


def basis_kernel(samp_ref, test_ref, coeffs_ref, *refs):
    parts, (basis_ref, proj_ref) = refs[:3], refs[3:]
    near_field = parts[0][...] + (parts[1][...] + parts[2][...])
    basis = dot3(samp_ref[...], coeffs_ref[...], NT) - near_field
    basis_ref[...] = basis
    proj_ref[...] = dot3(basis.T, test_ref[...])


def coupling(a, b):
    def norm3(v):
        return split3(v * v)

    ones = jnp.ones((RANK, DIM), BF16)
    inner = dot6(a, b, NT)
    na = sum(mm(p, ones, NT) for p in norm3(a))
    nb = sum(mm(ones, p, NT) for p in norm3(b))
    return jnp.exp2(-SCALE * (na + nb - 2.0 * inner))


EXT = SAMP + 2 * DIM
HALF = RANK // 2


def stack_node(lower, pick_own, skel_own, proj_own, pick_peer, skel_peer, proj_peer, stack_ref):
    def order(own, peer):
        return jnp.where(lower, own, peer), jnp.where(lower, peer, own)

    pick_a, pick_b = order(pick_own, pick_peer)
    proj_a, proj_b = order(proj_own, proj_peer)
    skel_a, skel_b = order(skel_own, skel_peer)
    stack_ref[0:RANK, :SAMP] = pick_a - dot3(coupling(skel_a[:, :DIM], skel_b[:, :DIM]), proj_b)
    stack_ref[RANK:, :SAMP] = pick_b - dot3(coupling(skel_b[:, :DIM], skel_a[:, :DIM]), proj_a)
    stack_ref[0:RANK, SAMP:] = skel_a
    stack_ref[RANK:, SAMP:] = skel_b


def picked_of(piv_ref, stack_ref):
    column = lax.broadcasted_iota(jnp.int32, (RANK, 2 * RANK), 1)
    one_hot = jnp.where(piv_ref[...] == column, 1.0, 0.0).astype(BF16)
    return pick(one_hot, stack_ref[...])


def half_of(lower, full):
    return jnp.where(lower, full[:HALF], full[HALF:])


def stack_kernel(
    info_ref, piv_ref, pick_own, skel_own, proj_own, pick_peer, skel_peer, proj_peer,
    stack_ref, picked_ref, skel_ref, send_ref
):
    lower = info_ref[0, 0] == 0
    stack_node(
        lower, pick_own[...], skel_own[...], proj_own[...],
        pick_peer[...], skel_peer[...], proj_peer[...], stack_ref,
    )
    picked = picked_of(piv_ref, stack_ref)
    picked_ref[...] = picked[:, :SAMP]
    skel_ref[...] = picked[:, SAMP:]
    send_ref[...] = half_of(lower, picked)


def mid_kernel(
    share, info_ref, stack_ref, picked_ref, proj_own, proj_peer, share_ref, proj_ref, send_ref, err_ref, inv_ref
):
    lower = info_ref[0, 0] == 0
    picked = picked_ref[...]
    coeffs = dot3(inverse_gram(picked, err_ref, inv_ref), picked)
    basis_t = dot3(coeffs, stack_ref[:, :SAMP], NT)
    left, right = basis_t[:, :RANK], basis_t[:, RANK:]
    proj = dot3(jnp.where(lower, left, right), proj_own[...]) + dot3(
        jnp.where(lower, right, left), proj_peer[...]
    )
    proj_ref[...] = proj
    send_ref[...] = half_of(lower, proj)
    rows = stack_ref[pl.ds(pl.multiple_of(info_ref[0, 1], 8), share), :SAMP]
    share_ref[...] = dot3(rows, coeffs, NT)


def top_kernel(
    share, info_ref, piv_ref, pick_own, skel_own, proj_own, pick_1, pick_2, proj_1, proj_2,
    share_ref, stack_ref, err_ref, inv_ref
):
    core0 = info_ref[0, 2] == 0

    def whole(first, second):
        f, o = first[...], second[...]
        return jnp.concatenate([jnp.where(core0, f, o), jnp.where(core0, o, f)], axis=0)

    peer = whole(pick_1, pick_2)
    stack_node(
        info_ref[0, 0] == 0, pick_own[...], skel_own[...], proj_own[...],
        peer[:, :SAMP], peer[:, SAMP:], whole(proj_1, proj_2), stack_ref,
    )
    picked = picked_of(piv_ref, stack_ref)[:, :SAMP]
    coeffs = dot3(inverse_gram(picked, err_ref, inv_ref), picked)
    rows = stack_ref[pl.ds(pl.multiple_of(info_ref[0, 1], 8), share), :SAMP]
    share_ref[...] = dot3(rows, coeffs, NT)


def after(first, *then):
    return lax.optimization_barrier((first, *then))


def sum_row(part, *then):
    share = part.shape[0] // 16
    parts = lax.all_to_all(part.reshape(16, share, -1), "row", 0, 0)
    mine, *then = after(jnp.sum(parts, axis=0), *then)
    every = lax.all_to_all(jnp.broadcast_to(mine[None], (16, *mine.shape)), "row", 0, 0)
    return (every.reshape(part.shape), *then)


def body(points, samples, test_matrix, near_mask, leaf_pivots, mid_pivots, top_pivots):
    leaf = lax.axis_index("leaf")
    row = lax.axis_index("row")
    core = leaf & 1
    start = (row * BLK).reshape(1, 1)
    xt = points.T
    pivots = leaf_pivots[0].reshape(RANK, 1)
    weight = jnp.where(core == 0, near_mask[0, 0], near_mask[0, 1]).astype(F32).reshape(1, 1)

    (skel,) = call(skel_kernel, [((RANK, 2 * DIM), F32)], 1, 2, name="skel")(start, pivots, xt)
    skel, message = after(skel, jnp.concatenate([test_matrix, xt], axis=0))
    own = [message]
    sib = [lax.ppermute(message, "leaf", SIBLING)]
    outer = [lax.ppermute(message, "leaf", OUTER)]
    own += [lax.ppermute(message, "row", shift(*by)) for by in SOURCE]
    skel, sib[0], outer[0], *own[1:] = sum_row(skel, sib[0], outer[0], *own[1:])
    (part,) = call(
        pivot_kernel, [((RANK, SAMP), F32)], 2, 6, [VMEM((4 * DIM, BLK), BF16)], name="pivot"
    )(start, weight, pivots, skel, samples, own[0], sib[0], outer[0])
    own[1:] = [jnp.concatenate(own[1:], axis=0)]
    sib.append(lax.ppermute(own[1], "leaf", SIBLING))
    outer.append(lax.ppermute(own[1], "leaf", OUTER))
    picked, xt = sum_row(part, xt)
    (feats,) = call(feature_kernel, [((SIDE, BLK, 4 * DIM), BF16)], 0, 4, name="features")(
        xt, *[lax.ppermute(xt, "row", shift(*by)) for by in TARGET]
    )
    (coeffs,) = call(
        solve_kernel, [((RANK, SAMP), F32)], 0, 1, SOLVE_SCRATCH, name="solve"
    )(picked)
    picked_sib = lax.ppermute(picked, "leaf", SIBLING)
    skel_sib = lax.ppermute(skel, "leaf", SIBLING)

    block = ((BLK, RANK), F32)
    sum_3, prods, rights = call(
        functools.partial(far_kernel, (3,)),
        [block] + [((COUNT, 2 * BLK, RANK), BF16), ((COUNT, 4 * DIM, BLK), BF16)], 1, 8,
        near_scratch((3,)), name="near_3", flops=10**10,
    )(weight, coeffs, feats, *own, *sib, *outer)
    got_3 = lax.ppermute(sum_3, "row", shift(*TARGET[2]))
    sum_1, sum_2 = call(
        functools.partial(near_kernel, (1, 2)), [block] * 2, 0, 3, near_scratch((1, 2)), name="near_12", flops=2 * 10**10,
    )(feats, prods, rights)
    got_3, picked_sib, skel_sib = after(got_3, picked_sib, skel_sib)
    got_1 = lax.ppermute(sum_1, "row", shift(*TARGET[0]))
    got_2 = lax.ppermute(sum_2, "row", shift(*TARGET[1]))
    (sum_0,) = call(
        functools.partial(near_kernel, (0,)), [block], 0, 4, near_scratch((0,)), name="near_0", flops=10**10
    )(feats, prods, rights, got_3)
    leaf_basis, proj = call(
        basis_kernel, [block, ((RANK, SAMP), F32)], 0, 6, name="basis", flops=10**9
    )(samples, test_matrix, coeffs, sum_0, got_1, got_2)
    (proj,) = sum_row(proj)
    proj_sib = lax.ppermute(proj, "leaf", SIBLING)

    def info(lower, first):
        return jnp.stack([lower, first, core]).astype(jnp.int32).reshape(1, 3)

    def row_of(table, node):
        return lax.dynamic_index_in_dim(table, node, 0, keepdims=False).reshape(RANK, 1)

    node = ((RANK, SAMP), F32)
    mid_share, top_share = RANK // 16, RANK // 32
    mid_info = info(core, core * RANK + row * mid_share)
    stack, picked, skel, send = call(
        stack_kernel, [((2 * RANK, EXT), F32), node, ((RANK, 2 * DIM), F32), ((HALF, EXT), F32)], 1, 7,
        name="mid_stack", flops=10**9,
    )(mid_info, row_of(mid_pivots, leaf >> 1), picked, skel, proj, picked_sib, skel_sib, proj_sib)
    pick_1 = lax.ppermute(send, "leaf", COUSIN)
    pick_2 = lax.ppermute(pick_1, "leaf", SIBLING)
    mid_basis, proj, send = call(
        functools.partial(mid_kernel, mid_share),
        [((mid_share, RANK), F32), node, ((HALF, SAMP), F32)], 1, 4, SOLVE_SCRATCH,
        name="mid_solve", flops=3 * 10**9,
    )(mid_info, stack, picked, proj, proj_sib)
    proj_1 = lax.ppermute(send, "leaf", COUSIN)
    proj_2 = lax.ppermute(proj_1, "leaf", SIBLING)
    second = leaf >> 1 & 1
    (top_basis,) = call(
        functools.partial(top_kernel, top_share), [((top_share, RANK), F32)], 1, 8,
        [VMEM((2 * RANK, EXT), F32), *SOLVE_SCRATCH], name="top", flops=3 * 10**9,
    )(
        info(second, second * RANK + core * (RANK // 2) + row * top_share), row_of(top_pivots, leaf >> 2),
        picked, skel, proj, pick_1, pick_2, proj_1, proj_2,
    )
    return (leaf_basis, mid_basis, top_basis)


def solution(mesh):
    split = P(("leaf", "row"), None)
    return jax.shard_map(
        body,
        mesh=mesh,
        in_specs=(split, split, split, P("leaf", None), P("leaf", None), P(), P()),
        out_specs=(split, split, split),
        check_vma=False,
    )
```

```python
import functools
import math

import jax
import jax.numpy as jnp
from jax import lax
from jax.experimental import pallas as pl
from jax.experimental.pallas import tpu as pltpu
from jax.sharding import PartitionSpec as P

DIM = 64
RANK = 256
SAMP = 512
BLK = 512
SIDE = 4
SCALE = math.log2(math.e) / DIM
HIGHEST = lax.Precision.HIGHEST
F32, BF16 = jnp.float32, jnp.bfloat16
VMEM = pltpu.VMEM


def shift(dx, dy):
    return [(4 * x + y, 4 * ((x + dx) % 4) + (y + dy) % 4) for x in range(4) for y in range(4)]


SIBLING = [(i, i ^ 1) for i in range(8)]
OUTER = [(1, 2), (2, 1), (3, 4), (4, 3), (5, 6), (6, 5)]
COUSIN = [(i, i ^ 2) for i in range(8)]


NN = (((1,), (0,)), ((), ()))
NT = (((1,), (1,)), ((), ()))


def mm(a, b, dims=NN):
    return lax.dot_general(a, b, dims, preferred_element_type=F32)


def split2(a):
    hi = a.astype(BF16)
    return hi, (a - hi.astype(F32)).astype(BF16)


def split3(a):
    hi = a.astype(BF16)
    rest = a - hi.astype(F32)
    mid = rest.astype(BF16)
    return hi, mid, (rest - mid.astype(F32)).astype(BF16)


def dot3(a, b, dims=NN):
    ah, al = split2(a)
    bh, bl = split2(b)
    return mm(ah, bh, dims) + (mm(ah, bl, dims) + mm(al, bh, dims))


def dot6(a, b, dims=NN):
    ah, am, al = split3(a)
    bh, bm, bl = split3(b)
    return mm(ah, bh, dims) + (
        (mm(ah, bm, dims) + mm(am, bh, dims))
        + (mm(am, bm, dims) + (mm(ah, bl, dims) + mm(al, bh, dims)))
    )


def pick(one_hot, a):
    h, m, l = split3(a)
    return (mm(one_hot, h) + mm(one_hot, m)) + mm(one_hot, l)


SOURCE = ((-1, 0), (0, -1), (1, 1))
TARGET = ((2, 0), (0, 2), (2, 2))


def norm_rows(xt, first):
    rows = lax.broadcasted_iota(jnp.int32, (DIM, BLK), 0)
    sq = jnp.sum(xt * xt, axis=0, keepdims=True) * (-SCALE)
    h, m, l = (v.astype(F32) for v in split3(sq))
    one = jnp.ones_like(sq)
    aux = jnp.zeros((DIM, BLK), F32)
    for n, part in enumerate((h, m, l, one, one, one) if first else (one, one, one, h, m, l)):
        aux = jnp.where(rows == n, part, aux)
    return aux


def left_features(xt):
    scaled = xt * (2.0 * SCALE)
    hi = scaled.astype(BF16).astype(F32)
    feat = jnp.concatenate([hi, hi, scaled - hi, norm_rows(xt, True)], axis=0)
    return feat.T.astype(BF16)


def right_features(xt, ref):
    hi, lo = split2(xt)
    ref[0:DIM, :] = hi
    ref[DIM:2 * DIM, :] = lo
    ref[2 * DIM:3 * DIM, :] = hi
    ref[3 * DIM:, :] = norm_rows(xt, False).astype(BF16)


def rows_of(start, piv_ref):
    column = lax.broadcasted_iota(jnp.int32, (RANK, BLK), 1)
    return jnp.where(piv_ref[...] == column + start, 1.0, 0.0).astype(BF16)


def pivot_kernel(
    row_ref, weight_ref, piv_ref, all_ref, samp_ref, own_ref, sib_ref, out_ref,
    feat_ref, part_ref, skel_ref, right_ref
):
    row = row_ref[0, 0]
    x, y = row >> 2, row & 3
    for i, (dx, dy) in enumerate(((0, 0),) + TARGET):
        feat_ref[i] = left_features(all_ref[(x + dx & 3) << 2 | (y + dy & 3)])
    got = jnp.zeros((RANK, 3 * DIM), F32)
    for r in range(16):
        got += mm(rows_of(r * BLK, piv_ref), jnp.concatenate(split3(all_ref[r]), axis=0), NT)
    skel = (got[:, :DIM] + got[:, DIM:2 * DIM]) + got[:, 2 * DIM:]
    skel_ref[...] = jnp.concatenate([skel, jnp.zeros((RANK, DIM), F32)], axis=1)
    scaled = skel * (2.0 * SCALE)
    hi = scaled.astype(BF16).astype(F32)
    lane = lax.broadcasted_iota(jnp.int32, (RANK, DIM), 1)
    sq = jnp.sum(skel * skel, axis=1, keepdims=True) * (-SCALE)
    aux = jnp.where(lane < 6, 1.0, 0.0)
    for n, part in enumerate(split3(sq)):
        aux = jnp.where(lane == n, part.astype(F32), aux)
    feat = jnp.concatenate([hi, hi, scaled - hi, aux], axis=1).astype(BF16)
    total = pick(rows_of(row * BLK, piv_ref), samp_ref[...])
    for n, ref in enumerate((own_ref, sib_ref, out_ref)):
        right_features(ref[BLK:, :], right_ref)
        kern = jnp.exp2(mm(feat, right_ref[...]))
        if n == 2:
            kern = kern * weight_ref[0, 0]
        total -= dot3(kern, ref[0:BLK, :])
    part_ref[...] = total


def near_steps(targets, feat_ref, groups, before, outs, acc, buf_a, buf_b):
    for i in range(len(targets)):
        acc[i] = before[i][...] if before else jnp.zeros((BLK, RANK), F32)
    for prod_ref, right_ref in groups:
        count = prod_ref.shape[0]
        total = len(targets) * count

        def entries(t, buf):
            k = jnp.exp2(mm(feat_ref[targets[0] + t // count], right_ref[t % count]))
            hi = k.astype(BF16)
            buf[:, BLK:] = hi
            buf[:, 0:BLK] = (k - hi.astype(F32)).astype(BF16)

        def fold(t, buf):
            b = t % count
            acc[t // count] += mm(buf[...], prod_ref[b]) + mm(buf[:, BLK:], prod_ref[b, 0:BLK, :])

        entries(0, buf_a)

        @pl.loop(0, total // 2)
        def _(u):
            t = 2 * u
            entries(t + 1, buf_b)
            fold(t, buf_a)
            entries(jnp.minimum(t + 2, total - 1), buf_a)
            fold(t + 1, buf_b)

    for i in range(len(targets)):
        outs[i][...] = acc[i]


def first_kernel(targets, count, weighted, weight_ref, coeffs_ref, feat_ref, *refs):
    n = len(targets)
    msgs, before = refs[:count], refs[count:-5 - n]
    outs, (prod_ref, right_ref), scratch = refs[-5 - n:-5], refs[-5:-3], refs[-3:]
    ch, cl = split2(coeffs_ref[...])
    for at, ref in enumerate(msgs):
        right_features(ref[BLK:, :], right_ref.at[at])
        test = ref[0:BLK, :]
        if weighted:
            test = test * weight_ref[0, 0]
        th, tl = split2(test)
        hi, lo = split2(mm(th, ch, NT) + (mm(th, cl, NT) + mm(tl, ch, NT)))
        prod_ref[at, 0:BLK, :] = hi
        prod_ref[at, BLK:, :] = lo
    near_steps(targets, feat_ref, [(prod_ref, right_ref)], before, outs, *scratch)


def next_kernel(targets, n_groups, feat_ref, *refs):
    n = len(targets)
    groups = [refs[2 * g:2 * g + 2] for g in range(n_groups)]
    before, outs, scratch = refs[2 * n_groups:-3 - n], refs[-3 - n:-3], refs[-3:]
    near_steps(targets, feat_ref, groups, before, outs, *scratch)


def call(kernel, outs, n_smem, n_vmem, scratch=(), name=None, flops=0, trans=0):
    return pl.pallas_call(
        kernel,
        out_shape=[jax.ShapeDtypeStruct(s, t) for s, t in outs],
        in_specs=[pl.BlockSpec(memory_space=pltpu.SMEM)] * n_smem
        + [pl.BlockSpec(memory_space=VMEM)] * n_vmem,
        out_specs=[pl.BlockSpec(memory_space=VMEM)] * len(outs),
        scratch_shapes=list(scratch),
        compiler_params=pltpu.CompilerParams(vmem_limit_bytes=50 * 2**20),
        cost_estimate=pl.CostEstimate(flops=flops, bytes_accessed=2**16, transcendentals=trans),
        name=name,
    )


def near_scratch(targets):
    return [VMEM((len(targets), BLK, RANK), F32), VMEM((BLK, 2 * BLK), BF16), VMEM((BLK, 2 * BLK), BF16)]


BLOCK = ((BLK, RANK), F32)


def first_near(name, targets, weight, coeffs, feats, msgs, before=(), weighted=False):
    count = len(msgs)
    *sums, prods, rights = call(
        functools.partial(first_kernel, targets, count, weighted),
        [BLOCK] * len(targets) + [((count, 2 * BLK, RANK), BF16), ((count, 4 * DIM, BLK), BF16)],
        1, 2 + count + len(before), near_scratch(targets), name=name, flops=10**10,
    )(weight, coeffs, feats, *msgs, *before)
    return sums, (prods, rights)


def next_near(name, targets, feats, groups, before):
    return call(
        functools.partial(next_kernel, targets, len(groups)),
        [BLOCK] * len(targets), 0, 1 + 2 * len(groups) + len(before), near_scratch(targets),
        name=name, flops=10**10,
    )(feats, *[v for g in groups for v in g], *before)


SOLVE_SCRATCH = [VMEM((RANK, RANK), F32), VMEM((RANK, RANK), F32)]


def inverse_gram(picked, err_ref, inv_ref):
    gram = dot6(picked, picked, NT)
    eye = (
        lax.broadcasted_iota(jnp.int32, (RANK, RANK), 0)
        == lax.broadcasted_iota(jnp.int32, (RANK, RANK), 1)
    ).astype(F32)
    shift = jnp.sum(gram * eye) / RANK + 1e-06
    gram = gram + shift * eye
    bound = jnp.max(jnp.sum(jnp.abs(gram), axis=0, keepdims=True))
    alpha = 2.0 / (jnp.full((1, 1), 1.0, F32) * (bound + shift))
    err_ref[...] = eye - alpha * gram
    inv_ref[...] = alpha * eye

    def step(state):
        n, _ = state
        err = err_ref[...]
        eh, el = split2(err)
        ih, il = split2(inv_ref[...])
        inv_ref[...] += mm(ih, eh) + (mm(ih, el) + mm(il, eh))
        sq = mm(eh, eh) + (mm(eh, el) + mm(el, eh))
        err_ref[...] = sq
        return n + 1, jnp.sum(sq * sq)

    lax.while_loop(lambda st: (st[0] < 24) & (st[1] > 1e-6), step, (jnp.int32(0), jnp.float32(1e9)))

    def correct(state):
        inv = inv_ref[...]
        err = eye - dot6(gram, inv)
        inv_ref[...] = inv + dot3(inv, err)
        return state[0] + 1, jnp.sum(err * err)

    lax.while_loop(lambda st: (st[0] < 4) & (st[1] > 1e-5), correct, (jnp.int32(0), jnp.float32(1e9)))
    return inv_ref[...]


def solve_kernel(picked_ref, coeffs_ref, err_ref, inv_ref):
    picked = picked_ref[...]
    coeffs_ref[...] = dot3(inverse_gram(picked, err_ref, inv_ref), picked)


def basis_kernel(samp_ref, test_ref, coeffs_ref, *refs):
    parts, (basis_ref, proj_ref) = refs[:3], refs[3:]
    near_field = parts[0][...] + (parts[1][...] + parts[2][...])
    basis = dot3(samp_ref[...], coeffs_ref[...], NT) - near_field
    basis_ref[...] = basis
    proj_ref[...] = dot3(basis.T, test_ref[...])


def coupling(a, b):
    def norm3(v):
        return split3(v * v)

    ones = jnp.ones((RANK, DIM), BF16)
    inner = dot6(a, b, NT)
    na = sum(mm(p, ones, NT) for p in norm3(a))
    nb = sum(mm(ones, p, NT) for p in norm3(b))
    return jnp.exp2(-SCALE * (na + nb - 2.0 * inner))


EXT = SAMP + 2 * DIM
HALF = RANK // 2


def stack_node(lower, pick_own, skel_own, proj_own, pick_peer, skel_peer, proj_peer, stack_ref):
    def order(own, peer):
        return jnp.where(lower, own, peer), jnp.where(lower, peer, own)

    pick_a, pick_b = order(pick_own, pick_peer)
    proj_a, proj_b = order(proj_own, proj_peer)
    skel_a, skel_b = order(skel_own, skel_peer)
    stack_ref[0:RANK, :SAMP] = pick_a - dot3(coupling(skel_a[:, :DIM], skel_b[:, :DIM]), proj_b)
    stack_ref[RANK:, :SAMP] = pick_b - dot3(coupling(skel_b[:, :DIM], skel_a[:, :DIM]), proj_a)
    stack_ref[0:RANK, SAMP:] = skel_a
    stack_ref[RANK:, SAMP:] = skel_b


def picked_of(piv_ref, stack_ref):
    column = lax.broadcasted_iota(jnp.int32, (RANK, 2 * RANK), 1)
    one_hot = jnp.where(piv_ref[...] == column, 1.0, 0.0).astype(BF16)
    return pick(one_hot, stack_ref[...])


def half_of(lower, full):
    return jnp.where(lower, full[:HALF], full[HALF:])


def stack_kernel(
    info_ref, piv_ref, pick_own, skel_own, proj_own, pick_peer, skel_peer, proj_peer,
    stack_ref, picked_ref, skel_ref, send_ref
):
    lower = info_ref[0, 0] == 0
    stack_node(
        lower, pick_own[...], skel_own[...], proj_own[...],
        pick_peer[...], skel_peer[...], proj_peer[...], stack_ref,
    )
    picked = picked_of(piv_ref, stack_ref)
    picked_ref[...] = picked[:, :SAMP]
    skel_ref[...] = picked[:, SAMP:]
    send_ref[...] = half_of(lower, picked)


def mid_kernel(
    share, info_ref, stack_ref, picked_ref, proj_own, proj_peer, share_ref, proj_ref, send_ref, err_ref, inv_ref
):
    lower = info_ref[0, 0] == 0
    picked = picked_ref[...]
    coeffs = dot3(inverse_gram(picked, err_ref, inv_ref), picked)
    basis_t = dot3(coeffs, stack_ref[:, :SAMP], NT)
    left, right = basis_t[:, :RANK], basis_t[:, RANK:]
    proj = dot3(jnp.where(lower, left, right), proj_own[...]) + dot3(
        jnp.where(lower, right, left), proj_peer[...]
    )
    proj_ref[...] = proj
    send_ref[...] = half_of(lower, proj)
    rows = stack_ref[pl.ds(pl.multiple_of(info_ref[0, 1], 8), share), :SAMP]
    share_ref[...] = dot3(rows, coeffs, NT)


def top_kernel(
    share, info_ref, piv_ref, pick_own, skel_own, proj_own, pick_1, pick_2, proj_1, proj_2,
    share_ref, stack_ref, err_ref, inv_ref
):
    core0 = info_ref[0, 2] == 0

    def whole(first, second):
        f, o = first[...], second[...]
        return jnp.concatenate([jnp.where(core0, f, o), jnp.where(core0, o, f)], axis=0)

    peer = whole(pick_1, pick_2)
    stack_node(
        info_ref[0, 0] == 0, pick_own[...], skel_own[...], proj_own[...],
        peer[:, :SAMP], peer[:, SAMP:], whole(proj_1, proj_2), stack_ref,
    )
    picked = picked_of(piv_ref, stack_ref)[:, :SAMP]
    coeffs = dot3(inverse_gram(picked, err_ref, inv_ref), picked)
    rows = stack_ref[pl.ds(pl.multiple_of(info_ref[0, 1], 8), share), :SAMP]
    share_ref[...] = dot3(rows, coeffs, NT)


def after(first, *then):
    return lax.optimization_barrier((first, *then))


def sum_row(part, *then):
    share = part.shape[0] // 16
    parts = lax.all_to_all(part.reshape(16, share, -1), "row", 0, 0)
    mine, *then = after(jnp.sum(parts, axis=0), *then)
    every = lax.all_to_all(jnp.broadcast_to(mine[None], (16, *mine.shape)), "row", 0, 0)
    return (every.reshape(part.shape), *then)


def body(points, samples, test_matrix, near_mask, leaf_pivots, mid_pivots, top_pivots):
    leaf = lax.axis_index("leaf")
    row = lax.axis_index("row")
    core = leaf & 1
    xt = points.T
    pivots = leaf_pivots[0].reshape(RANK, 1)
    weight = jnp.where(core == 0, near_mask[0, 0], near_mask[0, 1]).astype(F32).reshape(1, 1)

    message = jnp.concatenate([test_matrix, xt], axis=0)
    sib = [lax.ppermute(message, "leaf", SIBLING)]
    outer = [lax.ppermute(message, "leaf", OUTER)]
    points_all = lax.all_to_all(jnp.broadcast_to(xt[None], (16, DIM, BLK)), "row", 0, 0)
    points_all, late = after(points_all, message)
    own = [message] + [lax.ppermute(late, "row", shift(*by)) for by in SOURCE]
    feats, part, skel = call(
        pivot_kernel,
        [((SIDE, BLK, 4 * DIM), BF16), ((RANK, SAMP), F32), ((RANK, 2 * DIM), F32)], 2, 6,
        [VMEM((4 * DIM, BLK), BF16)], name="pivot",
    )(row.reshape(1, 1), weight, pivots, points_all, samples, own[0], sib[0], outer[0])
    picked, *own[1:] = sum_row(part, *own[1:])
    outer += [lax.ppermute(m, "leaf", OUTER) for m in own[1:]]
    sib += [lax.ppermute(m, "leaf", SIBLING) for m in own[1:]]
    (coeffs,) = call(
        solve_kernel, [((RANK, SAMP), F32)], 0, 1, SOLVE_SCRATCH, name="solve"
    )(picked)
    picked_sib = lax.ppermute(picked, "leaf", SIBLING)
    skel_sib = lax.ppermute(skel, "leaf", SIBLING)

    (sum_1, sum_2, sum_3), inner = first_near("near_inner", (1, 2, 3), weight, coeffs, feats, own + sib)
    feats, sum_1, sum_2, sum_3 = after(feats, sum_1, sum_2, sum_3)
    (sum_3,), outside = first_near("near_3", (3,), weight, coeffs, feats, outer, [sum_3], True)
    got_3 = lax.ppermute(sum_3, "row", shift(*TARGET[2]))
    sum_1, sum_2 = next_near("near_12", (1, 2), feats, [outside], [sum_1, sum_2])
    got_3, picked_sib, skel_sib = after(got_3, picked_sib, skel_sib)
    got_1 = lax.ppermute(sum_1, "row", shift(*TARGET[0]))
    got_2 = lax.ppermute(sum_2, "row", shift(*TARGET[1]))
    (sum_0,) = next_near("near_0", (0,), feats, [inner, outside], [got_3])
    leaf_basis, proj = call(
        basis_kernel, [BLOCK, ((RANK, SAMP), F32)], 0, 6, name="basis", flops=10**9
    )(samples, test_matrix, coeffs, sum_0, got_1, got_2)
    (proj,) = sum_row(proj)
    proj_sib = lax.ppermute(proj, "leaf", SIBLING)

    def info(lower, first):
        return jnp.stack([lower, first, core]).astype(jnp.int32).reshape(1, 3)

    def row_of(table, node):
        return lax.dynamic_index_in_dim(table, node, 0, keepdims=False).reshape(RANK, 1)

    node = ((RANK, SAMP), F32)
    mid_share, top_share = RANK // 16, RANK // 32
    mid_info = info(core, core * RANK + row * mid_share)
    stack, picked, skel, send = call(
        stack_kernel, [((2 * RANK, EXT), F32), node, ((RANK, 2 * DIM), F32), ((HALF, EXT), F32)], 1, 7,
        name="mid_stack", flops=10**9,
    )(mid_info, row_of(mid_pivots, leaf >> 1), picked, skel, proj, picked_sib, skel_sib, proj_sib)
    pick_1 = lax.ppermute(send, "leaf", COUSIN)
    pick_2 = lax.ppermute(pick_1, "leaf", SIBLING)
    mid_basis, proj, send = call(
        functools.partial(mid_kernel, mid_share),
        [((mid_share, RANK), F32), node, ((HALF, SAMP), F32)], 1, 4, SOLVE_SCRATCH,
        name="mid_solve", flops=3 * 10**9,
    )(mid_info, stack, picked, proj, proj_sib)
    proj_1 = lax.ppermute(send, "leaf", COUSIN)
    proj_2 = lax.ppermute(proj_1, "leaf", SIBLING)
    second = leaf >> 1 & 1
    (top_basis,) = call(
        functools.partial(top_kernel, top_share), [((top_share, RANK), F32)], 1, 8,
        [VMEM((2 * RANK, EXT), F32), *SOLVE_SCRATCH], name="top", flops=3 * 10**9,
    )(
        info(second, second * RANK + core * (RANK // 2) + row * top_share), row_of(top_pivots, leaf >> 2),
        picked, skel, proj, pick_1, pick_2, proj_1, proj_2,
    )
    return (leaf_basis, mid_basis, top_basis)


def solution(mesh):
    split = P(("leaf", "row"), None)
    return jax.shard_map(
        body,
        mesh=mesh,
        in_specs=(split, split, split, P("leaf", None), P("leaf", None), P(), P()),
        out_specs=(split, split, split),
        check_vma=False,
    )
```

```python
import functools
import math

import jax
import jax.numpy as jnp
from jax import lax
from jax.experimental import pallas as pl
from jax.experimental.pallas import tpu as pltpu
from jax.sharding import PartitionSpec as P

DIM = 64
RANK = 256
SAMP = 512
BLK = 512
SIDE = 4
SCALE = math.log2(math.e) / DIM
HIGHEST = lax.Precision.HIGHEST
F32, BF16 = jnp.float32, jnp.bfloat16
VMEM = pltpu.VMEM


def shift(dx, dy):
    return [(4 * x + y, 4 * ((x + dx) % 4) + (y + dy) % 4) for x in range(4) for y in range(4)]


SIBLING = [(i, i ^ 1) for i in range(8)]
OUTER = [(1, 2), (2, 1), (3, 4), (4, 3), (5, 6), (6, 5)]
COUSIN = [(i, i ^ 2) for i in range(8)]


NN = (((1,), (0,)), ((), ()))
NT = (((1,), (1,)), ((), ()))


def mm(a, b, dims=NN):
    return lax.dot_general(a, b, dims, preferred_element_type=F32)


def split2(a):
    hi = a.astype(BF16)
    return hi, (a - hi.astype(F32)).astype(BF16)


def split3(a):
    hi = a.astype(BF16)
    rest = a - hi.astype(F32)
    mid = rest.astype(BF16)
    return hi, mid, (rest - mid.astype(F32)).astype(BF16)


def dot3(a, b, dims=NN):
    ah, al = split2(a)
    bh, bl = split2(b)
    return mm(ah, bh, dims) + (mm(ah, bl, dims) + mm(al, bh, dims))


def dot6(a, b, dims=NN):
    ah, am, al = split3(a)
    bh, bm, bl = split3(b)
    return mm(ah, bh, dims) + (
        (mm(ah, bm, dims) + mm(am, bh, dims))
        + (mm(am, bm, dims) + (mm(ah, bl, dims) + mm(al, bh, dims)))
    )


def pick(one_hot, a):
    h, m, l = split3(a)
    return (mm(one_hot, h) + mm(one_hot, m)) + mm(one_hot, l)


SOURCE = ((-1, 0), (0, -1), (1, 1))
TARGET = ((2, 0), (0, 2), (2, 2))


def norm_rows(xt, first):
    rows = lax.broadcasted_iota(jnp.int32, (DIM, BLK), 0)
    sq = jnp.sum(xt * xt, axis=0, keepdims=True) * (-SCALE)
    h, m, l = (v.astype(F32) for v in split3(sq))
    one = jnp.ones_like(sq)
    aux = jnp.zeros((DIM, BLK), F32)
    for n, part in enumerate((h, m, l, one, one, one) if first else (one, one, one, h, m, l)):
        aux = jnp.where(rows == n, part, aux)
    return aux


def left_features(xt):
    scaled = xt * (2.0 * SCALE)
    hi = scaled.astype(BF16).astype(F32)
    feat = jnp.concatenate([hi, hi, scaled - hi, norm_rows(xt, True)], axis=0)
    return feat.T.astype(BF16)


def right_features(xt, ref):
    hi, lo = split2(xt)
    ref[0:DIM, :] = hi
    ref[DIM:2 * DIM, :] = lo
    ref[2 * DIM:3 * DIM, :] = hi
    ref[3 * DIM:, :] = norm_rows(xt, False).astype(BF16)


def rows_of(start, piv_ref):
    column = lax.broadcasted_iota(jnp.int32, (RANK, BLK), 1)
    return jnp.where(piv_ref[...] == column + start, 1.0, 0.0).astype(BF16)


def pivot_kernel(
    row_ref, weight_ref, piv_ref, all_ref, samp_ref, own_ref, sib_ref, out_ref,
    feat_ref, part_ref, skel_ref, right_ref
):
    row = row_ref[0, 0]
    x, y = row >> 2, row & 3
    for i, (dx, dy) in enumerate(((0, 0),) + TARGET):
        feat_ref[i] = left_features(all_ref[(x + dx & 3) << 2 | (y + dy & 3)])
    got = jnp.zeros((RANK, 3 * DIM), F32)
    for r in range(16):
        got += mm(rows_of(r * BLK, piv_ref), jnp.concatenate(split3(all_ref[r]), axis=0), NT)
    skel = (got[:, :DIM] + got[:, DIM:2 * DIM]) + got[:, 2 * DIM:]
    skel_ref[...] = jnp.concatenate([skel, jnp.zeros((RANK, DIM), F32)], axis=1)
    scaled = skel * (2.0 * SCALE)
    hi = scaled.astype(BF16).astype(F32)
    lane = lax.broadcasted_iota(jnp.int32, (RANK, DIM), 1)
    sq = jnp.sum(skel * skel, axis=1, keepdims=True) * (-SCALE)
    aux = jnp.where(lane < 6, 1.0, 0.0)
    for n, part in enumerate(split3(sq)):
        aux = jnp.where(lane == n, part.astype(F32), aux)
    feat = jnp.concatenate([hi, hi, scaled - hi, aux], axis=1).astype(BF16)
    total = pick(rows_of(row * BLK, piv_ref), samp_ref[...])
    for n, ref in enumerate((own_ref, sib_ref, out_ref)):
        right_features(ref[BLK:, :], right_ref)
        kern = jnp.exp2(mm(feat, right_ref[...]))
        if n == 2:
            kern = kern * weight_ref[0, 0]
        total -= dot3(kern, ref[0:BLK, :])
    part_ref[...] = total


def near_steps(targets, feat_ref, groups, before, outs, acc, buf_a, buf_b):
    for i in range(len(targets)):
        acc[i] = before[i][...] if before else jnp.zeros((BLK, RANK), F32)
    for ref in before[len(targets):]:
        acc[0] += ref[...]
    for prod_ref, right_ref in groups:
        count = prod_ref.shape[0]
        total = len(targets) * count

        def entries(t, buf):
            k = jnp.exp2(mm(feat_ref[targets[0] + t // count], right_ref[t % count]))
            hi = k.astype(BF16)
            buf[:, BLK:] = hi
            buf[:, 0:BLK] = (k - hi.astype(F32)).astype(BF16)

        def fold(t, buf):
            b = t % count
            acc[t // count] += mm(buf[...], prod_ref[b]) + mm(buf[:, BLK:], prod_ref[b, 0:BLK, :])

        entries(0, buf_a)

        @pl.loop(0, total // 2)
        def _(u):
            t = 2 * u
            entries(t + 1, buf_b)
            fold(t, buf_a)
            entries(jnp.minimum(t + 2, total - 1), buf_a)
            fold(t + 1, buf_b)

        if total % 2:
            fold(total - 1, buf_a)

    for i in range(len(targets)):
        outs[i][...] = acc[i]


def first_kernel(targets, count, weighted, weight_ref, coeffs_ref, feat_ref, *refs):
    n = len(targets)
    msgs, before = refs[:count], refs[count:-5 - n]
    outs, (prod_ref, right_ref), scratch = refs[-5 - n:-5], refs[-5:-3], refs[-3:]
    ch, cl = split2(coeffs_ref[...])
    for at, ref in enumerate(msgs):
        right_features(ref[BLK:, :], right_ref.at[at])
        test = ref[0:BLK, :]
        if at in weighted:
            test = test * weight_ref[0, 0]
        th, tl = split2(test)
        hi, lo = split2(mm(th, ch, NT) + (mm(th, cl, NT) + mm(tl, ch, NT)))
        prod_ref[at, 0:BLK, :] = hi
        prod_ref[at, BLK:, :] = lo
    near_steps(targets, feat_ref, [(prod_ref, right_ref)], before, outs, *scratch)


def next_kernel(targets, n_groups, feat_ref, *refs):
    n = len(targets)
    groups = [refs[2 * g:2 * g + 2] for g in range(n_groups)]
    before, outs, scratch = refs[2 * n_groups:-3 - n], refs[-3 - n:-3], refs[-3:]
    near_steps(targets, feat_ref, groups, before, outs, *scratch)


def call(kernel, outs, n_smem, n_vmem, scratch=(), name=None, flops=0, trans=0):
    return pl.pallas_call(
        kernel,
        out_shape=[jax.ShapeDtypeStruct(s, t) for s, t in outs],
        in_specs=[pl.BlockSpec(memory_space=pltpu.SMEM)] * n_smem
        + [pl.BlockSpec(memory_space=VMEM)] * n_vmem,
        out_specs=[pl.BlockSpec(memory_space=VMEM)] * len(outs),
        scratch_shapes=list(scratch),
        compiler_params=pltpu.CompilerParams(vmem_limit_bytes=50 * 2**20),
        cost_estimate=pl.CostEstimate(flops=flops, bytes_accessed=2**16, transcendentals=trans),
        name=name,
    )


def near_scratch(targets):
    return [VMEM((len(targets), BLK, RANK), F32), VMEM((BLK, 2 * BLK), BF16), VMEM((BLK, 2 * BLK), BF16)]


BLOCK = ((BLK, RANK), F32)


def first_near(name, targets, weight, coeffs, feats, msgs, before=(), weighted=()):
    count = len(msgs)
    *sums, prods, rights = call(
        functools.partial(first_kernel, targets, count, weighted),
        [BLOCK] * len(targets) + [((count, 2 * BLK, RANK), BF16), ((count, 4 * DIM, BLK), BF16)],
        1, 2 + count + len(before), near_scratch(targets), name=name, flops=10**10,
    )(weight, coeffs, feats, *msgs, *before)
    return sums, (prods, rights)


def next_near(name, targets, feats, groups, before):
    return call(
        functools.partial(next_kernel, targets, len(groups)),
        [BLOCK] * len(targets), 0, 1 + 2 * len(groups) + len(before), near_scratch(targets),
        name=name, flops=10**10,
    )(feats, *[v for g in groups for v in g], *before)


SOLVE_SCRATCH = [VMEM((RANK, RANK), F32), VMEM((RANK, RANK), F32)]


def inverse_gram(picked, err_ref, inv_ref):
    gram = dot6(picked, picked, NT)
    eye = (
        lax.broadcasted_iota(jnp.int32, (RANK, RANK), 0)
        == lax.broadcasted_iota(jnp.int32, (RANK, RANK), 1)
    ).astype(F32)
    shift = jnp.sum(gram * eye) / RANK + 1e-06
    gram = gram + shift * eye
    bound = jnp.max(jnp.sum(jnp.abs(gram), axis=0, keepdims=True))
    alpha = 2.0 / (jnp.full((1, 1), 1.0, F32) * (bound + shift))
    err_ref[...] = eye - alpha * gram
    inv_ref[...] = alpha * eye

    def step(state):
        n, _ = state
        err = err_ref[...]
        eh, el = split2(err)
        ih, il = split2(inv_ref[...])
        inv_ref[...] += mm(ih, eh) + (mm(ih, el) + mm(il, eh))
        sq = mm(eh, eh) + (mm(eh, el) + mm(el, eh))
        err_ref[...] = sq
        return n + 1, jnp.sum(sq * sq)

    lax.while_loop(lambda st: (st[0] < 24) & (st[1] > 1e-6), step, (jnp.int32(0), jnp.float32(1e9)))

    def correct(state):
        inv = inv_ref[...]
        err = eye - dot6(gram, inv)
        inv_ref[...] = inv + dot3(inv, err)
        return state[0] + 1, jnp.sum(err * err)

    lax.while_loop(lambda st: (st[0] < 4) & (st[1] > 1e-5), correct, (jnp.int32(0), jnp.float32(1e9)))
    return inv_ref[...]


def solve_kernel(picked_ref, coeffs_ref, err_ref, inv_ref):
    picked = picked_ref[...]
    coeffs_ref[...] = dot3(inverse_gram(picked, err_ref, inv_ref), picked)


def basis_kernel(samp_ref, test_ref, coeffs_ref, *refs):
    parts, (basis_ref, proj_ref) = refs[:3], refs[3:]
    near_field = parts[0][...] + (parts[1][...] + parts[2][...])
    basis = dot3(samp_ref[...], coeffs_ref[...], NT) - near_field
    basis_ref[...] = basis
    proj_ref[...] = dot3(basis.T, test_ref[...])


def coupling(a, b):
    def norm3(v):
        return split3(v * v)

    ones = jnp.ones((RANK, DIM), BF16)
    inner = dot6(a, b, NT)
    na = sum(mm(p, ones, NT) for p in norm3(a))
    nb = sum(mm(ones, p, NT) for p in norm3(b))
    return jnp.exp2(-SCALE * (na + nb - 2.0 * inner))


EXT = SAMP + 2 * DIM
HALF = RANK // 2


def stack_node(lower, pick_own, skel_own, proj_own, pick_peer, skel_peer, proj_peer, stack_ref):
    def order(own, peer):
        return jnp.where(lower, own, peer), jnp.where(lower, peer, own)

    pick_a, pick_b = order(pick_own, pick_peer)
    proj_a, proj_b = order(proj_own, proj_peer)
    skel_a, skel_b = order(skel_own, skel_peer)
    stack_ref[0:RANK, :SAMP] = pick_a - dot3(coupling(skel_a[:, :DIM], skel_b[:, :DIM]), proj_b)
    stack_ref[RANK:, :SAMP] = pick_b - dot3(coupling(skel_b[:, :DIM], skel_a[:, :DIM]), proj_a)
    stack_ref[0:RANK, SAMP:] = skel_a
    stack_ref[RANK:, SAMP:] = skel_b


def picked_of(piv_ref, stack_ref):
    column = lax.broadcasted_iota(jnp.int32, (RANK, 2 * RANK), 1)
    one_hot = jnp.where(piv_ref[...] == column, 1.0, 0.0).astype(BF16)
    return pick(one_hot, stack_ref[...])


def half_of(lower, full):
    return jnp.where(lower, full[:HALF], full[HALF:])


def stack_kernel(
    info_ref, piv_ref, pick_own, skel_own, proj_own, pick_peer, skel_peer, proj_peer,
    stack_ref, picked_ref, skel_ref, send_ref
):
    lower = info_ref[0, 0] == 0
    stack_node(
        lower, pick_own[...], skel_own[...], proj_own[...],
        pick_peer[...], skel_peer[...], proj_peer[...], stack_ref,
    )
    picked = picked_of(piv_ref, stack_ref)
    picked_ref[...] = picked[:, :SAMP]
    skel_ref[...] = picked[:, SAMP:]
    send_ref[...] = half_of(lower, picked)


def mid_kernel(
    share, info_ref, stack_ref, picked_ref, proj_own, proj_peer, share_ref, proj_ref, send_ref, err_ref, inv_ref
):
    lower = info_ref[0, 0] == 0
    picked = picked_ref[...]
    coeffs = dot3(inverse_gram(picked, err_ref, inv_ref), picked)
    basis_t = dot3(coeffs, stack_ref[:, :SAMP], NT)
    left, right = basis_t[:, :RANK], basis_t[:, RANK:]
    proj = dot3(jnp.where(lower, left, right), proj_own[...]) + dot3(
        jnp.where(lower, right, left), proj_peer[...]
    )
    proj_ref[...] = proj
    send_ref[...] = half_of(lower, proj)
    rows = stack_ref[pl.ds(pl.multiple_of(info_ref[0, 1], 8), share), :SAMP]
    share_ref[...] = dot3(rows, coeffs, NT)


def top_kernel(
    share, info_ref, piv_ref, pick_own, skel_own, proj_own, pick_1, pick_2, proj_1, proj_2,
    share_ref, stack_ref, err_ref, inv_ref
):
    core0 = info_ref[0, 2] == 0

    def whole(first, second):
        f, o = first[...], second[...]
        return jnp.concatenate([jnp.where(core0, f, o), jnp.where(core0, o, f)], axis=0)

    peer = whole(pick_1, pick_2)
    stack_node(
        info_ref[0, 0] == 0, pick_own[...], skel_own[...], proj_own[...],
        peer[:, :SAMP], peer[:, SAMP:], whole(proj_1, proj_2), stack_ref,
    )
    picked = picked_of(piv_ref, stack_ref)[:, :SAMP]
    coeffs = dot3(inverse_gram(picked, err_ref, inv_ref), picked)
    rows = stack_ref[pl.ds(pl.multiple_of(info_ref[0, 1], 8), share), :SAMP]
    share_ref[...] = dot3(rows, coeffs, NT)


def after(first, *then):
    return lax.optimization_barrier((first, *then))


def sum_row(part, *then):
    share = part.shape[0] // 16
    parts = lax.all_to_all(part.reshape(16, share, -1), "row", 0, 0)
    mine, *then = after(jnp.sum(parts, axis=0), *then)
    every = lax.all_to_all(jnp.broadcast_to(mine[None], (16, *mine.shape)), "row", 0, 0)
    return (every.reshape(part.shape), *then)


def body(points, samples, test_matrix, near_mask, leaf_pivots, mid_pivots, top_pivots):
    leaf = lax.axis_index("leaf")
    row = lax.axis_index("row")
    core = leaf & 1
    xt = points.T
    pivots = leaf_pivots[0].reshape(RANK, 1)
    weight = jnp.where(core == 0, near_mask[0, 0], near_mask[0, 1]).astype(F32).reshape(1, 1)

    message = jnp.concatenate([test_matrix, xt], axis=0)
    sib = [lax.ppermute(message, "leaf", SIBLING)]
    outer = [lax.ppermute(message, "leaf", OUTER)]
    points_all = lax.all_to_all(jnp.broadcast_to(xt[None], (16, DIM, BLK)), "row", 0, 0)
    feats, part, skel = call(
        pivot_kernel,
        [((SIDE, BLK, 4 * DIM), BF16), ((RANK, SAMP), F32), ((RANK, 2 * DIM), F32)], 2, 6,
        [VMEM((4 * DIM, BLK), BF16)], name="pivot",
    )(row.reshape(1, 1), weight, pivots, points_all, samples, message, sib[0], outer[0])
    picked, late = sum_row(part, message)
    far = [lax.ppermute(late, "row", shift(*by)) for by in SOURCE]
    (coeffs,) = call(
        solve_kernel, [((RANK, SAMP), F32)], 0, 1, SOLVE_SCRATCH, name="solve"
    )(picked)
    picked_sib = lax.ppermute(picked, "leaf", SIBLING)
    skel_sib = lax.ppermute(skel, "leaf", SIBLING)

    (sum_0, *sums), _ = first_near(
        "near_local", (0, 1, 2, 3), weight, coeffs, feats, [message, sib[0], outer[0]], weighted=(2,)
    )
    sum_0, *far = after(sum_0, *far)
    sib = [lax.ppermute(m, "leaf", SIBLING) for m in far]
    outer = [lax.ppermute(m, "leaf", OUTER) for m in far]
    (sum_1, sum_2, sum_3), inner = first_near(
        "near_inner", (1, 2, 3), weight, coeffs, feats, far + sib, sums
    )
    (sum_3,), outside = first_near("near_3", (3,), weight, coeffs, feats, outer, [sum_3], (0, 1, 2))
    got_3 = lax.ppermute(sum_3, "row", shift(*TARGET[2]))
    sum_1, sum_2 = next_near("near_12", (1, 2), feats, [outside], [sum_1, sum_2])
    got_3, picked_sib, skel_sib = after(got_3, picked_sib, skel_sib)
    got_1 = lax.ppermute(sum_1, "row", shift(*TARGET[0]))
    got_2 = lax.ppermute(sum_2, "row", shift(*TARGET[1]))
    (sum_0,) = next_near("near_0", (0,), feats, [inner, outside], [sum_0, got_3])
    leaf_basis, proj = call(
        basis_kernel, [BLOCK, ((RANK, SAMP), F32)], 0, 6, name="basis", flops=10**9
    )(samples, test_matrix, coeffs, sum_0, got_1, got_2)
    (proj,) = sum_row(proj)
    proj_sib = lax.ppermute(proj, "leaf", SIBLING)

    def info(lower, first):
        return jnp.stack([lower, first, core]).astype(jnp.int32).reshape(1, 3)

    def row_of(table, node):
        return lax.dynamic_index_in_dim(table, node, 0, keepdims=False).reshape(RANK, 1)

    node = ((RANK, SAMP), F32)
    mid_share, top_share = RANK // 16, RANK // 32
    mid_info = info(core, core * RANK + row * mid_share)
    stack, picked, skel, send = call(
        stack_kernel, [((2 * RANK, EXT), F32), node, ((RANK, 2 * DIM), F32), ((HALF, EXT), F32)], 1, 7,
        name="mid_stack", flops=10**9,
    )(mid_info, row_of(mid_pivots, leaf >> 1), picked, skel, proj, picked_sib, skel_sib, proj_sib)
    pick_1 = lax.ppermute(send, "leaf", COUSIN)
    pick_2 = lax.ppermute(pick_1, "leaf", SIBLING)
    mid_basis, proj, send = call(
        functools.partial(mid_kernel, mid_share),
        [((mid_share, RANK), F32), node, ((HALF, SAMP), F32)], 1, 4, SOLVE_SCRATCH,
        name="mid_solve", flops=3 * 10**9,
    )(mid_info, stack, picked, proj, proj_sib)
    proj_1 = lax.ppermute(send, "leaf", COUSIN)
    proj_2 = lax.ppermute(proj_1, "leaf", SIBLING)
    second = leaf >> 1 & 1
    (top_basis,) = call(
        functools.partial(top_kernel, top_share), [((top_share, RANK), F32)], 1, 8,
        [VMEM((2 * RANK, EXT), F32), *SOLVE_SCRATCH], name="top", flops=3 * 10**9,
    )(
        info(second, second * RANK + core * (RANK // 2) + row * top_share), row_of(top_pivots, leaf >> 2),
        picked, skel, proj, pick_1, pick_2, proj_1, proj_2,
    )
    return (leaf_basis, mid_basis, top_basis)


def solution(mesh):
    split = P(("leaf", "row"), None)
    return jax.shard_map(
        body,
        mesh=mesh,
        in_specs=(split, split, split, P("leaf", None), P("leaf", None), P(), P()),
        out_specs=(split, split, split),
        check_vma=False,
    )
```

```python
import functools
import math

import jax
import jax.numpy as jnp
from jax import lax
from jax.experimental import pallas as pl
from jax.experimental.pallas import tpu as pltpu
from jax.sharding import PartitionSpec as P

DIM = 64
RANK = 256
SAMP = 512
BLK = 512
SIDE = 4
SCALE = math.log2(math.e) / DIM
HIGHEST = lax.Precision.HIGHEST
F32, BF16 = jnp.float32, jnp.bfloat16
VMEM = pltpu.VMEM


def shift(dx, dy):
    return [(4 * x + y, 4 * ((x + dx) % 4) + (y + dy) % 4) for x in range(4) for y in range(4)]


SIBLING = [(i, i ^ 1) for i in range(8)]
OUTER = [(1, 2), (2, 1), (3, 4), (4, 3), (5, 6), (6, 5)]
COUSIN = [(i, i ^ 2) for i in range(8)]


NN = (((1,), (0,)), ((), ()))
NT = (((1,), (1,)), ((), ()))


def mm(a, b, dims=NN):
    return lax.dot_general(a, b, dims, preferred_element_type=F32)


def split2(a):
    hi = a.astype(BF16)
    return hi, (a - hi.astype(F32)).astype(BF16)


def split3(a):
    hi = a.astype(BF16)
    rest = a - hi.astype(F32)
    mid = rest.astype(BF16)
    return hi, mid, (rest - mid.astype(F32)).astype(BF16)


def dot3(a, b, dims=NN):
    ah, al = split2(a)
    bh, bl = split2(b)
    return mm(ah, bh, dims) + (mm(ah, bl, dims) + mm(al, bh, dims))


def dot6(a, b, dims=NN):
    ah, am, al = split3(a)
    bh, bm, bl = split3(b)
    return mm(ah, bh, dims) + (
        (mm(ah, bm, dims) + mm(am, bh, dims))
        + (mm(am, bm, dims) + (mm(ah, bl, dims) + mm(al, bh, dims)))
    )


def pick(one_hot, a):
    h, m, l = split3(a)
    return (mm(one_hot, h) + mm(one_hot, m)) + mm(one_hot, l)


SOURCE = ((-1, 0), (0, -1), (1, 1))
TARGET = ((2, 0), (0, 2), (2, 2))


def norm_rows(xt, first):
    rows = lax.broadcasted_iota(jnp.int32, (DIM, BLK), 0)
    sq = jnp.sum(xt * xt, axis=0, keepdims=True) * (-SCALE)
    h, m, l = (v.astype(F32) for v in split3(sq))
    one = jnp.ones_like(sq)
    aux = jnp.zeros((DIM, BLK), F32)
    for n, part in enumerate((h, m, l, one, one, one) if first else (one, one, one, h, m, l)):
        aux = jnp.where(rows == n, part, aux)
    return aux


def left_features(xt):
    scaled = xt * (2.0 * SCALE)
    hi = scaled.astype(BF16).astype(F32)
    feat = jnp.concatenate([hi, hi, scaled - hi, norm_rows(xt, True)], axis=0)
    return feat.T.astype(BF16)


def right_features(xt, ref):
    hi, lo = split2(xt)
    ref[0:DIM, :] = hi
    ref[DIM:2 * DIM, :] = lo
    ref[2 * DIM:3 * DIM, :] = hi
    ref[3 * DIM:, :] = norm_rows(xt, False).astype(BF16)


def rows_of(start, piv_ref):
    column = lax.broadcasted_iota(jnp.int32, (RANK, BLK), 1)
    return jnp.where(piv_ref[...] == column + start, 1.0, 0.0).astype(BF16)


def skel_kernel(start_ref, piv_ref, points_ref, skel_ref):
    one_hot = rows_of(start_ref[0, 0], piv_ref)
    skel = sum(mm(one_hot, part, NT) for part in split3(points_ref[...]))
    skel_ref[...] = jnp.concatenate([skel, jnp.zeros((RANK, DIM), F32)], axis=1)


def feature_kernel(p0, p1, p2, p3, feat_ref):
    for i, ref in enumerate((p0, p1, p2, p3)):
        feat_ref[i] = left_features(ref[...])


def pivot_kernel(
    start_ref, weight_ref, piv_ref, skel_ref, samp_ref, own_ref, sib_ref, out_ref, part_ref, right_ref
):
    skel = skel_ref[:, :DIM]
    scaled = skel * (2.0 * SCALE)
    hi = scaled.astype(BF16).astype(F32)
    lane = lax.broadcasted_iota(jnp.int32, (RANK, DIM), 1)
    sq = jnp.sum(skel * skel, axis=1, keepdims=True) * (-SCALE)
    aux = jnp.where(lane < 6, 1.0, 0.0)
    for n, part in enumerate(split3(sq)):
        aux = jnp.where(lane == n, part.astype(F32), aux)
    feat = jnp.concatenate([hi, hi, scaled - hi, aux], axis=1).astype(BF16)
    total = pick(rows_of(start_ref[0, 0], piv_ref), samp_ref[...])
    for n, ref in enumerate((own_ref, sib_ref, out_ref)):
        right_features(ref[BLK:, :], right_ref)
        kern = jnp.exp2(mm(feat, right_ref[...]))
        if n == 2:
            kern = kern * weight_ref[0, 0]
        total -= dot3(kern, ref[0:BLK, :])
    part_ref[...] = total


def near_steps(targets, feat_ref, groups, before, outs, acc, buf_a, buf_b):
    for i in range(len(targets)):
        acc[i] = before[i][...] if before else jnp.zeros((BLK, RANK), F32)
    for prod_ref, right_ref in groups:
        count = prod_ref.shape[0]
        total = len(targets) * count

        def entries(t, buf):
            k = jnp.exp2(mm(feat_ref[targets[0] + t // count], right_ref[t % count]))
            hi = k.astype(BF16)
            buf[:, BLK:] = hi
            buf[:, 0:BLK] = (k - hi.astype(F32)).astype(BF16)

        def fold(t, buf):
            b = t % count
            acc[t // count] += mm(buf[...], prod_ref[b]) + mm(buf[:, BLK:], prod_ref[b, 0:BLK, :])

        entries(0, buf_a)

        @pl.loop(0, total // 2)
        def _(u):
            t = 2 * u
            entries(t + 1, buf_b)
            fold(t, buf_a)
            entries(jnp.minimum(t + 2, total - 1), buf_a)
            fold(t + 1, buf_b)

    for i in range(len(targets)):
        outs[i][...] = acc[i]


def first_kernel(targets, count, weighted, weight_ref, coeffs_ref, feat_ref, *refs):
    n = len(targets)
    msgs, before = refs[:count], refs[count:-5 - n]
    outs, (prod_ref, right_ref), scratch = refs[-5 - n:-5], refs[-5:-3], refs[-3:]
    ch, cl = split2(coeffs_ref[...])
    for at, ref in enumerate(msgs):
        right_features(ref[BLK:, :], right_ref.at[at])
        test = ref[0:BLK, :]
        if weighted:
            test = test * weight_ref[0, 0]
        th, tl = split2(test)
        hi, lo = split2(mm(th, ch, NT) + (mm(th, cl, NT) + mm(tl, ch, NT)))
        prod_ref[at, 0:BLK, :] = hi
        prod_ref[at, BLK:, :] = lo
    near_steps(targets, feat_ref, [(prod_ref, right_ref)], before, outs, *scratch)


def next_kernel(targets, n_groups, feat_ref, *refs):
    n = len(targets)
    groups = [refs[2 * g:2 * g + 2] for g in range(n_groups)]
    before, outs, scratch = refs[2 * n_groups:-3 - n], refs[-3 - n:-3], refs[-3:]
    near_steps(targets, feat_ref, groups, before, outs, *scratch)


def call(kernel, outs, n_smem, n_vmem, scratch=(), name=None, flops=0, trans=0):
    return pl.pallas_call(
        kernel,
        out_shape=[jax.ShapeDtypeStruct(s, t) for s, t in outs],
        in_specs=[pl.BlockSpec(memory_space=pltpu.SMEM)] * n_smem
        + [pl.BlockSpec(memory_space=VMEM)] * n_vmem,
        out_specs=[pl.BlockSpec(memory_space=VMEM)] * len(outs),
        scratch_shapes=list(scratch),
        compiler_params=pltpu.CompilerParams(vmem_limit_bytes=50 * 2**20),
        cost_estimate=pl.CostEstimate(flops=flops, bytes_accessed=2**16, transcendentals=trans),
        name=name,
    )


def near_scratch(targets):
    return [VMEM((len(targets), BLK, RANK), F32), VMEM((BLK, 2 * BLK), BF16), VMEM((BLK, 2 * BLK), BF16)]


BLOCK = ((BLK, RANK), F32)


def first_near(name, targets, weight, coeffs, feats, msgs, before=(), weighted=False):
    count = len(msgs)
    *sums, prods, rights = call(
        functools.partial(first_kernel, targets, count, weighted),
        [BLOCK] * len(targets) + [((count, 2 * BLK, RANK), BF16), ((count, 4 * DIM, BLK), BF16)],
        1, 2 + count + len(before), near_scratch(targets), name=name, flops=10**10,
    )(weight, coeffs, feats, *msgs, *before)
    return sums, (prods, rights)


def next_near(name, targets, feats, groups, before):
    return call(
        functools.partial(next_kernel, targets, len(groups)),
        [BLOCK] * len(targets), 0, 1 + 2 * len(groups) + len(before), near_scratch(targets),
        name=name, flops=10**10,
    )(feats, *[v for g in groups for v in g], *before)


SOLVE_SCRATCH = [VMEM((RANK, RANK), F32), VMEM((RANK, RANK), F32)]


def inverse_gram(picked, err_ref, inv_ref):
    gram = dot6(picked, picked, NT)
    eye = (
        lax.broadcasted_iota(jnp.int32, (RANK, RANK), 0)
        == lax.broadcasted_iota(jnp.int32, (RANK, RANK), 1)
    ).astype(F32)
    shift = jnp.sum(gram * eye) / RANK + 1e-06
    gram = gram + shift * eye
    bound = jnp.max(jnp.sum(jnp.abs(gram), axis=0, keepdims=True))
    alpha = 2.0 / (jnp.full((1, 1), 1.0, F32) * (bound + shift))
    err_ref[...] = eye - alpha * gram
    inv_ref[...] = alpha * eye

    def step(state):
        n, _ = state
        err = err_ref[...]
        eh, el = split2(err)
        ih, il = split2(inv_ref[...])
        inv_ref[...] += mm(ih, eh) + (mm(ih, el) + mm(il, eh))
        sq = mm(eh, eh) + (mm(eh, el) + mm(el, eh))
        err_ref[...] = sq
        return n + 1, jnp.sum(sq * sq)

    lax.while_loop(lambda st: (st[0] < 24) & (st[1] > 1e-6), step, (jnp.int32(0), jnp.float32(1e9)))

    def correct(state):
        inv = inv_ref[...]
        err = eye - dot6(gram, inv)
        inv_ref[...] = inv + dot3(inv, err)
        return state[0] + 1, jnp.sum(err * err)

    lax.while_loop(lambda st: (st[0] < 4) & (st[1] > 1e-5), correct, (jnp.int32(0), jnp.float32(1e9)))
    return inv_ref[...]


def solve_kernel(picked_ref, coeffs_ref, err_ref, inv_ref):
    picked = picked_ref[...]
    coeffs_ref[...] = dot3(inverse_gram(picked, err_ref, inv_ref), picked)


def basis_kernel(samp_ref, test_ref, coeffs_ref, *refs):
    parts, (basis_ref, proj_ref) = refs[:3], refs[3:]
    near_field = parts[0][...] + (parts[1][...] + parts[2][...])
    basis = dot3(samp_ref[...], coeffs_ref[...], NT) - near_field
    basis_ref[...] = basis
    proj_ref[...] = dot3(basis.T, test_ref[...])


def coupling(a, b):
    def norm3(v):
        return split3(v * v)

    ones = jnp.ones((RANK, DIM), BF16)
    inner = dot6(a, b, NT)
    na = sum(mm(p, ones, NT) for p in norm3(a))
    nb = sum(mm(ones, p, NT) for p in norm3(b))
    return jnp.exp2(-SCALE * (na + nb - 2.0 * inner))


EXT = SAMP + 2 * DIM
HALF = RANK // 2


def stack_node(lower, pick_own, skel_own, proj_own, pick_peer, skel_peer, proj_peer, stack_ref):
    def order(own, peer):
        return jnp.where(lower, own, peer), jnp.where(lower, peer, own)

    pick_a, pick_b = order(pick_own, pick_peer)
    proj_a, proj_b = order(proj_own, proj_peer)
    skel_a, skel_b = order(skel_own, skel_peer)
    stack_ref[0:RANK, :SAMP] = pick_a - dot3(coupling(skel_a[:, :DIM], skel_b[:, :DIM]), proj_b)
    stack_ref[RANK:, :SAMP] = pick_b - dot3(coupling(skel_b[:, :DIM], skel_a[:, :DIM]), proj_a)
    stack_ref[0:RANK, SAMP:] = skel_a
    stack_ref[RANK:, SAMP:] = skel_b


def picked_of(piv_ref, stack_ref):
    column = lax.broadcasted_iota(jnp.int32, (RANK, 2 * RANK), 1)
    one_hot = jnp.where(piv_ref[...] == column, 1.0, 0.0).astype(BF16)
    return pick(one_hot, stack_ref[...])


def half_of(lower, full):
    return jnp.where(lower, full[:HALF], full[HALF:])


def stack_kernel(
    info_ref, piv_ref, pick_own, skel_own, proj_own, pick_peer, skel_peer, proj_peer,
    stack_ref, picked_ref, skel_ref, send_ref
):
    lower = info_ref[0, 0] == 0
    stack_node(
        lower, pick_own[...], skel_own[...], proj_own[...],
        pick_peer[...], skel_peer[...], proj_peer[...], stack_ref,
    )
    picked = picked_of(piv_ref, stack_ref)
    picked_ref[...] = picked[:, :SAMP]
    skel_ref[...] = picked[:, SAMP:]
    send_ref[...] = half_of(lower, picked)


def mid_kernel(
    share, info_ref, stack_ref, picked_ref, proj_own, proj_peer, share_ref, proj_ref, send_ref, err_ref, inv_ref
):
    lower = info_ref[0, 0] == 0
    picked = picked_ref[...]
    coeffs = dot3(inverse_gram(picked, err_ref, inv_ref), picked)
    basis_t = dot3(coeffs, stack_ref[:, :SAMP], NT)
    left, right = basis_t[:, :RANK], basis_t[:, RANK:]
    proj = dot3(jnp.where(lower, left, right), proj_own[...]) + dot3(
        jnp.where(lower, right, left), proj_peer[...]
    )
    proj_ref[...] = proj
    send_ref[...] = half_of(lower, proj)
    rows = stack_ref[pl.ds(pl.multiple_of(info_ref[0, 1], 8), share), :SAMP]
    share_ref[...] = dot3(rows, coeffs, NT)


def top_kernel(
    share, info_ref, piv_ref, pick_own, skel_own, proj_own, pick_1, pick_2, proj_1, proj_2,
    share_ref, stack_ref, err_ref, inv_ref
):
    core0 = info_ref[0, 2] == 0

    def whole(first, second):
        f, o = first[...], second[...]
        return jnp.concatenate([jnp.where(core0, f, o), jnp.where(core0, o, f)], axis=0)

    peer = whole(pick_1, pick_2)
    stack_node(
        info_ref[0, 0] == 0, pick_own[...], skel_own[...], proj_own[...],
        peer[:, :SAMP], peer[:, SAMP:], whole(proj_1, proj_2), stack_ref,
    )
    picked = picked_of(piv_ref, stack_ref)[:, :SAMP]
    coeffs = dot3(inverse_gram(picked, err_ref, inv_ref), picked)
    rows = stack_ref[pl.ds(pl.multiple_of(info_ref[0, 1], 8), share), :SAMP]
    share_ref[...] = dot3(rows, coeffs, NT)


def after(first, *then):
    return lax.optimization_barrier((first, *then))


def sum_row(part, *then):
    share = part.shape[0] // 16
    parts = lax.all_to_all(part.reshape(16, share, -1), "row", 0, 0)
    mine, *then = after(jnp.sum(parts, axis=0), *then)
    every = lax.all_to_all(jnp.broadcast_to(mine[None], (16, *mine.shape)), "row", 0, 0)
    return (every.reshape(part.shape), *then)


def body(points, samples, test_matrix, near_mask, leaf_pivots, mid_pivots, top_pivots):
    leaf = lax.axis_index("leaf")
    row = lax.axis_index("row")
    core = leaf & 1
    xt = points.T
    pivots = leaf_pivots[0].reshape(RANK, 1)
    weight = jnp.where(core == 0, near_mask[0, 0], near_mask[0, 1]).astype(F32).reshape(1, 1)

    message = jnp.concatenate([test_matrix, xt], axis=0)
    sib = [lax.ppermute(message, "leaf", SIBLING)]
    outer = [lax.ppermute(message, "leaf", OUTER)]
    start = (row * BLK).reshape(1, 1)
    (skel,) = call(skel_kernel, [((RANK, 2 * DIM), F32)], 1, 2, name="skel")(start, pivots, xt)
    (skel,) = sum_row(skel)
    skel, late = after(skel, message)
    own = [message] + [lax.ppermute(late, "row", shift(*by)) for by in SOURCE]
    (part,) = call(
        pivot_kernel, [((RANK, SAMP), F32)], 2, 6, [VMEM((4 * DIM, BLK), BF16)], name="pivot"
    )(start, weight, pivots, skel, samples, own[0], sib[0], outer[0])
    part, xt = after(part, xt)
    targets = [lax.ppermute(xt, "row", shift(*by)) for by in TARGET]
    picked, *rest = sum_row(part, *own[1:], *targets)
    own[1:], targets = rest[:3], rest[3:]
    (feats,) = call(feature_kernel, [((SIDE, BLK, 4 * DIM), BF16)], 0, 4, name="features")(xt, *targets)
    outer += [lax.ppermute(m, "leaf", OUTER) for m in own[1:]]
    sib += [lax.ppermute(m, "leaf", SIBLING) for m in own[1:]]
    (coeffs,) = call(
        solve_kernel, [((RANK, SAMP), F32)], 0, 1, SOLVE_SCRATCH, name="solve"
    )(picked)
    picked_sib = lax.ppermute(picked, "leaf", SIBLING)
    skel_sib = lax.ppermute(skel, "leaf", SIBLING)

    (sum_1, sum_2, sum_3), inner = first_near("near_inner", (1, 2, 3), weight, coeffs, feats, own + sib)
    feats, sum_1, sum_2, sum_3 = after(feats, sum_1, sum_2, sum_3)
    (sum_3,), outside = first_near("near_3", (3,), weight, coeffs, feats, outer, [sum_3], True)
    got_3 = lax.ppermute(sum_3, "row", shift(*TARGET[2]))
    sum_1, sum_2 = next_near("near_12", (1, 2), feats, [outside], [sum_1, sum_2])
    got_3, picked_sib, skel_sib = after(got_3, picked_sib, skel_sib)
    got_1 = lax.ppermute(sum_1, "row", shift(*TARGET[0]))
    got_2 = lax.ppermute(sum_2, "row", shift(*TARGET[1]))
    (sum_0,) = next_near("near_0", (0,), feats, [inner, outside], [got_3])
    leaf_basis, proj = call(
        basis_kernel, [BLOCK, ((RANK, SAMP), F32)], 0, 6, name="basis", flops=10**9
    )(samples, test_matrix, coeffs, sum_0, got_1, got_2)
    (proj,) = sum_row(proj)
    proj_sib = lax.ppermute(proj, "leaf", SIBLING)

    def info(lower, first):
        return jnp.stack([lower, first, core]).astype(jnp.int32).reshape(1, 3)

    def row_of(table, node):
        return lax.dynamic_index_in_dim(table, node, 0, keepdims=False).reshape(RANK, 1)

    node = ((RANK, SAMP), F32)
    mid_share, top_share = RANK // 16, RANK // 32
    mid_info = info(core, core * RANK + row * mid_share)
    stack, picked, skel, send = call(
        stack_kernel, [((2 * RANK, EXT), F32), node, ((RANK, 2 * DIM), F32), ((HALF, EXT), F32)], 1, 7,
        name="mid_stack", flops=10**9,
    )(mid_info, row_of(mid_pivots, leaf >> 1), picked, skel, proj, picked_sib, skel_sib, proj_sib)
    pick_1 = lax.ppermute(send, "leaf", COUSIN)
    pick_2 = lax.ppermute(pick_1, "leaf", SIBLING)
    mid_basis, proj, send = call(
        functools.partial(mid_kernel, mid_share),
        [((mid_share, RANK), F32), node, ((HALF, SAMP), F32)], 1, 4, SOLVE_SCRATCH,
        name="mid_solve", flops=3 * 10**9,
    )(mid_info, stack, picked, proj, proj_sib)
    proj_1 = lax.ppermute(send, "leaf", COUSIN)
    proj_2 = lax.ppermute(proj_1, "leaf", SIBLING)
    second = leaf >> 1 & 1
    (top_basis,) = call(
        functools.partial(top_kernel, top_share), [((top_share, RANK), F32)], 1, 8,
        [VMEM((2 * RANK, EXT), F32), *SOLVE_SCRATCH], name="top", flops=3 * 10**9,
    )(
        info(second, second * RANK + core * (RANK // 2) + row * top_share), row_of(top_pivots, leaf >> 2),
        picked, skel, proj, pick_1, pick_2, proj_1, proj_2,
    )
    return (leaf_basis, mid_basis, top_basis)


def solution(mesh):
    split = P(("leaf", "row"), None)
    return jax.shard_map(
        body,
        mesh=mesh,
        in_specs=(split, split, split, P("leaf", None), P("leaf", None), P(), P()),
        out_specs=(split, split, split),
        check_vma=False,
    )
```

```python
import functools
import math

import jax
import jax.numpy as jnp
from jax import lax
from jax.experimental import pallas as pl
from jax.experimental.pallas import tpu as pltpu
from jax.sharding import PartitionSpec as P

DIM = 64
RANK = 256
SAMP = 512
BLK = 512
SIDE = 4
SCALE = math.log2(math.e) / DIM
HIGHEST = lax.Precision.HIGHEST
F32, BF16 = jnp.float32, jnp.bfloat16
VMEM = pltpu.VMEM


def shift(dx, dy):
    return [(4 * x + y, 4 * ((x + dx) % 4) + (y + dy) % 4) for x in range(4) for y in range(4)]


SIBLING = [(i, i ^ 1) for i in range(8)]
OUTER = [(1, 2), (2, 1), (3, 4), (4, 3), (5, 6), (6, 5)]
COUSIN = [(i, i ^ 2) for i in range(8)]


NN = (((1,), (0,)), ((), ()))
NT = (((1,), (1,)), ((), ()))


def mm(a, b, dims=NN):
    return lax.dot_general(a, b, dims, preferred_element_type=F32)


def split2(a):
    hi = a.astype(BF16)
    return hi, (a - hi.astype(F32)).astype(BF16)


def split3(a):
    hi = a.astype(BF16)
    rest = a - hi.astype(F32)
    mid = rest.astype(BF16)
    return hi, mid, (rest - mid.astype(F32)).astype(BF16)


def dot3(a, b, dims=NN):
    ah, al = split2(a)
    bh, bl = split2(b)
    return mm(ah, bh, dims) + (mm(ah, bl, dims) + mm(al, bh, dims))


def dot6(a, b, dims=NN):
    ah, am, al = split3(a)
    bh, bm, bl = split3(b)
    return mm(ah, bh, dims) + (
        (mm(ah, bm, dims) + mm(am, bh, dims))
        + (mm(am, bm, dims) + (mm(ah, bl, dims) + mm(al, bh, dims)))
    )


def pick(one_hot, a):
    h, m, l = split3(a)
    return (mm(one_hot, h) + mm(one_hot, m)) + mm(one_hot, l)


SOURCE = ((-1, 0), (0, -1), (1, 1))
TARGET = ((2, 0), (0, 2), (2, 2))


def norm_rows(xt, first):
    rows = lax.broadcasted_iota(jnp.int32, (DIM, BLK), 0)
    sq = jnp.sum(xt * xt, axis=0, keepdims=True) * (-SCALE)
    h, m, l = (v.astype(F32) for v in split3(sq))
    one = jnp.ones_like(sq)
    aux = jnp.zeros((DIM, BLK), F32)
    for n, part in enumerate((h, m, l, one, one, one) if first else (one, one, one, h, m, l)):
        aux = jnp.where(rows == n, part, aux)
    return aux


def left_features(xt):
    scaled = xt * (2.0 * SCALE)
    hi = scaled.astype(BF16).astype(F32)
    feat = jnp.concatenate([hi, hi, scaled - hi, norm_rows(xt, True)], axis=0)
    return feat.T.astype(BF16)


def right_features(xt, ref):
    hi, lo = split2(xt)
    ref[0:DIM, :] = hi
    ref[DIM:2 * DIM, :] = lo
    ref[2 * DIM:3 * DIM, :] = hi
    ref[3 * DIM:, :] = norm_rows(xt, False).astype(BF16)


def rows_of(start, piv_ref):
    column = lax.broadcasted_iota(jnp.int32, (RANK, BLK), 1)
    return jnp.where(piv_ref[...] == column + start, 1.0, 0.0).astype(BF16)


def skel_kernel(start_ref, piv_ref, points_ref, skel_ref):
    one_hot = rows_of(start_ref[0, 0], piv_ref)
    skel = sum(mm(one_hot, part, NT) for part in split3(points_ref[...]))
    skel_ref[...] = jnp.concatenate([skel, jnp.zeros((RANK, DIM), F32)], axis=1)


def feature_kernel(p0, p1, p2, p3, feat_ref):
    for i, ref in enumerate((p0, p1, p2, p3)):
        feat_ref[i] = left_features(ref[...])


def pivot_kernel(
    start_ref, weight_ref, piv_ref, skel_ref, samp_ref, own_ref, sib_ref, out_ref, part_ref, right_ref
):
    skel = skel_ref[:, :DIM]
    scaled = skel * (2.0 * SCALE)
    hi = scaled.astype(BF16).astype(F32)
    lane = lax.broadcasted_iota(jnp.int32, (RANK, DIM), 1)
    sq = jnp.sum(skel * skel, axis=1, keepdims=True) * (-SCALE)
    aux = jnp.where(lane < 6, 1.0, 0.0)
    for n, part in enumerate(split3(sq)):
        aux = jnp.where(lane == n, part.astype(F32), aux)
    feat = jnp.concatenate([hi, hi, scaled - hi, aux], axis=1).astype(BF16)
    total = pick(rows_of(start_ref[0, 0], piv_ref), samp_ref[...])
    for n, ref in enumerate((own_ref, sib_ref, out_ref)):
        right_features(ref[BLK:, :], right_ref)
        kern = jnp.exp2(mm(feat, right_ref[...]))
        if n == 2:
            kern = kern * weight_ref[0, 0]
        total -= dot3(kern, ref[0:BLK, :])
    part_ref[...] = total


def near_steps(targets, feat_ref, groups, before, outs, acc, buf_a, buf_b):
    for i in range(len(targets)):
        acc[i] = before[i][...] if before else jnp.zeros((BLK, RANK), F32)
    for prod_ref, right_ref in groups:
        count = prod_ref.shape[0]
        total = len(targets) * count

        def entries(t, buf):
            k = jnp.exp2(mm(feat_ref[targets[0] + t // count], right_ref[t % count]))
            hi = k.astype(BF16)
            buf[:, BLK:] = hi
            buf[:, 0:BLK] = (k - hi.astype(F32)).astype(BF16)

        def fold(t, buf):
            b = t % count
            acc[t // count] += mm(buf[...], prod_ref[b]) + mm(buf[:, BLK:], prod_ref[b, 0:BLK, :])

        entries(0, buf_a)

        @pl.loop(0, total // 2)
        def _(u):
            t = 2 * u
            entries(t + 1, buf_b)
            fold(t, buf_a)
            entries(jnp.minimum(t + 2, total - 1), buf_a)
            fold(t + 1, buf_b)

    for i in range(len(targets)):
        outs[i][...] = acc[i]


def first_kernel(targets, count, weighted, weight_ref, coeffs_ref, feat_ref, *refs):
    n = len(targets)
    msgs, before = refs[:count], refs[count:-5 - n]
    outs, (prod_ref, right_ref), scratch = refs[-5 - n:-5], refs[-5:-3], refs[-3:]
    ch, cl = split2(coeffs_ref[...])
    for at, ref in enumerate(msgs):
        right_features(ref[BLK:, :], right_ref.at[at])
        test = ref[0:BLK, :]
        if weighted:
            test = test * weight_ref[0, 0]
        th, tl = split2(test)
        hi, lo = split2(mm(th, ch, NT) + (mm(th, cl, NT) + mm(tl, ch, NT)))
        prod_ref[at, 0:BLK, :] = hi
        prod_ref[at, BLK:, :] = lo
    near_steps(targets, feat_ref, [(prod_ref, right_ref)], before, outs, *scratch)


def next_kernel(targets, n_groups, feat_ref, *refs):
    n = len(targets)
    groups = [refs[2 * g:2 * g + 2] for g in range(n_groups)]
    before, outs, scratch = refs[2 * n_groups:-3 - n], refs[-3 - n:-3], refs[-3:]
    near_steps(targets, feat_ref, groups, before, outs, *scratch)


def call(kernel, outs, n_smem, n_vmem, scratch=(), name=None, flops=0, trans=0):
    return pl.pallas_call(
        kernel,
        out_shape=[jax.ShapeDtypeStruct(s, t) for s, t in outs],
        in_specs=[pl.BlockSpec(memory_space=pltpu.SMEM)] * n_smem
        + [pl.BlockSpec(memory_space=VMEM)] * n_vmem,
        out_specs=[pl.BlockSpec(memory_space=VMEM)] * len(outs),
        scratch_shapes=list(scratch),
        compiler_params=pltpu.CompilerParams(vmem_limit_bytes=50 * 2**20),
        cost_estimate=pl.CostEstimate(flops=flops, bytes_accessed=2**16, transcendentals=trans),
        name=name,
    )


def near_scratch(targets):
    return [VMEM((len(targets), BLK, RANK), F32), VMEM((BLK, 2 * BLK), BF16), VMEM((BLK, 2 * BLK), BF16)]


BLOCK = ((BLK, RANK), F32)


def first_near(name, targets, weight, coeffs, feats, msgs, before=(), weighted=False):
    count = len(msgs)
    *sums, prods, rights = call(
        functools.partial(first_kernel, targets, count, weighted),
        [BLOCK] * len(targets) + [((count, 2 * BLK, RANK), BF16), ((count, 4 * DIM, BLK), BF16)],
        1, 2 + count + len(before), near_scratch(targets), name=name, flops=10**10,
    )(weight, coeffs, feats, *msgs, *before)
    return sums, (prods, rights)


def next_near(name, targets, feats, groups, before):
    return call(
        functools.partial(next_kernel, targets, len(groups)),
        [BLOCK] * len(targets), 0, 1 + 2 * len(groups) + len(before), near_scratch(targets),
        name=name, flops=10**10,
    )(feats, *[v for g in groups for v in g], *before)


SOLVE_SCRATCH = [VMEM((RANK, RANK), F32), VMEM((RANK, RANK), F32)]


def inverse_gram(picked, err_ref, inv_ref):
    gram = dot6(picked, picked, NT)
    eye = (
        lax.broadcasted_iota(jnp.int32, (RANK, RANK), 0)
        == lax.broadcasted_iota(jnp.int32, (RANK, RANK), 1)
    ).astype(F32)
    shift = jnp.sum(gram * eye) / RANK + 1e-06
    gram = gram + shift * eye
    bound = jnp.max(jnp.sum(jnp.abs(gram), axis=0, keepdims=True))
    alpha = 2.0 / (jnp.full((1, 1), 1.0, F32) * (bound + shift))
    err_ref[...] = eye - alpha * gram
    inv_ref[...] = alpha * eye

    def step(state):
        n, _ = state
        err = err_ref[...]
        eh, el = split2(err)
        ih, il = split2(inv_ref[...])
        inv_ref[...] += mm(ih, eh) + (mm(ih, el) + mm(il, eh))
        sq = mm(eh, eh) + (mm(eh, el) + mm(el, eh))
        err_ref[...] = sq
        return n + 1, jnp.sum(sq * sq)

    lax.while_loop(lambda st: (st[0] < 24) & (st[1] > 1e-6), step, (jnp.int32(0), jnp.float32(1e9)))

    def correct(state):
        inv = inv_ref[...]
        err = eye - dot6(gram, inv)
        inv_ref[...] = inv + dot3(inv, err)
        return state[0] + 1, jnp.sum(err * err)

    lax.while_loop(lambda st: (st[0] < 4) & (st[1] > 1e-5), correct, (jnp.int32(0), jnp.float32(1e9)))
    return inv_ref[...]


def solve_kernel(picked_ref, coeffs_ref, err_ref, inv_ref):
    picked = picked_ref[...]
    coeffs_ref[...] = dot3(inverse_gram(picked, err_ref, inv_ref), picked)


def basis_kernel(samp_ref, test_ref, coeffs_ref, *refs):
    parts, (basis_ref, proj_ref) = refs[:3], refs[3:]
    near_field = parts[0][...] + (parts[1][...] + parts[2][...])
    basis = dot3(samp_ref[...], coeffs_ref[...], NT) - near_field
    basis_ref[...] = basis
    proj_ref[...] = dot3(basis.T, test_ref[...])


def coupling(a, b):
    def norm3(v):
        return split3(v * v)

    ones = jnp.ones((RANK, DIM), BF16)
    inner = dot6(a, b, NT)
    na = sum(mm(p, ones, NT) for p in norm3(a))
    nb = sum(mm(ones, p, NT) for p in norm3(b))
    return jnp.exp2(-SCALE * (na + nb - 2.0 * inner))


EXT = SAMP + 2 * DIM
HALF = RANK // 2


def stack_node(lower, pick_own, skel_own, proj_own, pick_peer, skel_peer, proj_peer, stack_ref):
    def order(own, peer):
        return jnp.where(lower, own, peer), jnp.where(lower, peer, own)

    pick_a, pick_b = order(pick_own, pick_peer)
    proj_a, proj_b = order(proj_own, proj_peer)
    skel_a, skel_b = order(skel_own, skel_peer)
    stack_ref[0:RANK, :SAMP] = pick_a - dot3(coupling(skel_a[:, :DIM], skel_b[:, :DIM]), proj_b)
    stack_ref[RANK:, :SAMP] = pick_b - dot3(coupling(skel_b[:, :DIM], skel_a[:, :DIM]), proj_a)
    stack_ref[0:RANK, SAMP:] = skel_a
    stack_ref[RANK:, SAMP:] = skel_b


def picked_of(piv_ref, stack_ref):
    column = lax.broadcasted_iota(jnp.int32, (RANK, 2 * RANK), 1)
    one_hot = jnp.where(piv_ref[...] == column, 1.0, 0.0).astype(BF16)
    return pick(one_hot, stack_ref[...])


def half_of(lower, full):
    return jnp.where(lower, full[:HALF], full[HALF:])


def stack_kernel(
    info_ref, piv_ref, pick_own, skel_own, proj_own, pick_peer, skel_peer, proj_peer,
    stack_ref, picked_ref, skel_ref, send_ref
):
    lower = info_ref[0, 0] == 0
    stack_node(
        lower, pick_own[...], skel_own[...], proj_own[...],
        pick_peer[...], skel_peer[...], proj_peer[...], stack_ref,
    )
    picked = picked_of(piv_ref, stack_ref)
    picked_ref[...] = picked[:, :SAMP]
    skel_ref[...] = picked[:, SAMP:]
    send_ref[...] = half_of(lower, picked)


def mid_kernel(
    share, info_ref, stack_ref, picked_ref, proj_own, proj_peer, share_ref, proj_ref, send_ref, err_ref, inv_ref
):
    lower = info_ref[0, 0] == 0
    picked = picked_ref[...]
    coeffs = dot3(inverse_gram(picked, err_ref, inv_ref), picked)
    basis_t = dot3(coeffs, stack_ref[:, :SAMP], NT)
    left, right = basis_t[:, :RANK], basis_t[:, RANK:]
    proj = dot3(jnp.where(lower, left, right), proj_own[...]) + dot3(
        jnp.where(lower, right, left), proj_peer[...]
    )
    proj_ref[...] = proj
    send_ref[...] = half_of(lower, proj)
    rows = stack_ref[pl.ds(pl.multiple_of(info_ref[0, 1], 8), share), :SAMP]
    share_ref[...] = dot3(rows, coeffs, NT)


def top_kernel(
    share, info_ref, piv_ref, pick_own, skel_own, proj_own, pick_1, pick_2, proj_1, proj_2,
    share_ref, stack_ref, err_ref, inv_ref
):
    core0 = info_ref[0, 2] == 0

    def whole(first, second):
        f, o = first[...], second[...]
        return jnp.concatenate([jnp.where(core0, f, o), jnp.where(core0, o, f)], axis=0)

    peer = whole(pick_1, pick_2)
    stack_node(
        info_ref[0, 0] == 0, pick_own[...], skel_own[...], proj_own[...],
        peer[:, :SAMP], peer[:, SAMP:], whole(proj_1, proj_2), stack_ref,
    )
    picked = picked_of(piv_ref, stack_ref)[:, :SAMP]
    coeffs = dot3(inverse_gram(picked, err_ref, inv_ref), picked)
    rows = stack_ref[pl.ds(pl.multiple_of(info_ref[0, 1], 8), share), :SAMP]
    share_ref[...] = dot3(rows, coeffs, NT)


def after(first, *then):
    return lax.optimization_barrier((first, *then))


def sum_row(part, *then):
    share = part.shape[0] // 16
    parts = lax.all_to_all(part.reshape(16, share, -1), "row", 0, 0)
    mine, *then = after(jnp.sum(parts, axis=0), *then)
    every = lax.all_to_all(jnp.broadcast_to(mine[None], (16, *mine.shape)), "row", 0, 0)
    return (every.reshape(part.shape), *then)


def body(points, samples, test_matrix, near_mask, leaf_pivots, mid_pivots, top_pivots):
    leaf = lax.axis_index("leaf")
    row = lax.axis_index("row")
    core = leaf & 1
    xt = points.T
    pivots = leaf_pivots[0].reshape(RANK, 1)
    weight = jnp.where(core == 0, near_mask[0, 0], near_mask[0, 1]).astype(F32).reshape(1, 1)

    message = jnp.concatenate([test_matrix, xt], axis=0)
    sib = [lax.ppermute(message, "leaf", SIBLING)]
    outer = [lax.ppermute(message, "leaf", OUTER)]
    start = (row * BLK).reshape(1, 1)
    (skel,) = call(skel_kernel, [((RANK, 2 * DIM), F32)], 1, 2, name="skel")(start, pivots, xt)
    targets = [lax.ppermute(xt, "row", shift(*by)) for by in TARGET]
    skel, *targets = sum_row(skel, *targets)
    skel, late = after(skel, message)
    own = [message] + [lax.ppermute(late, "row", shift(*by)) for by in SOURCE]
    (part,) = call(
        pivot_kernel, [((RANK, SAMP), F32)], 2, 6, [VMEM((4 * DIM, BLK), BF16)], name="pivot"
    )(start, weight, pivots, skel, samples, own[0], sib[0], outer[0])
    picked, *own[1:] = sum_row(part, *own[1:])
    (feats,) = call(feature_kernel, [((SIDE, BLK, 4 * DIM), BF16)], 0, 4, name="features")(xt, *targets)
    outer += [lax.ppermute(m, "leaf", OUTER) for m in own[1:]]
    sib += [lax.ppermute(m, "leaf", SIBLING) for m in own[1:]]
    (coeffs,) = call(
        solve_kernel, [((RANK, SAMP), F32)], 0, 1, SOLVE_SCRATCH, name="solve"
    )(picked)
    picked_sib = lax.ppermute(picked, "leaf", SIBLING)
    skel_sib = lax.ppermute(skel, "leaf", SIBLING)

    (sum_1, sum_2, sum_3), inner = first_near("near_inner", (1, 2, 3), weight, coeffs, feats, own + sib)
    feats, sum_1, sum_2, sum_3 = after(feats, sum_1, sum_2, sum_3)
    (sum_3,), outside = first_near("near_3", (3,), weight, coeffs, feats, outer, [sum_3], True)
    got_3 = lax.ppermute(sum_3, "row", shift(*TARGET[2]))
    sum_1, sum_2 = next_near("near_12", (1, 2), feats, [outside], [sum_1, sum_2])
    got_3, picked_sib, skel_sib = after(got_3, picked_sib, skel_sib)
    got_1 = lax.ppermute(sum_1, "row", shift(*TARGET[0]))
    got_2 = lax.ppermute(sum_2, "row", shift(*TARGET[1]))
    (sum_0,) = next_near("near_0", (0,), feats, [inner, outside], [got_3])
    leaf_basis, proj = call(
        basis_kernel, [BLOCK, ((RANK, SAMP), F32)], 0, 6, name="basis", flops=10**9
    )(samples, test_matrix, coeffs, sum_0, got_1, got_2)
    (proj,) = sum_row(proj)
    proj_sib = lax.ppermute(proj, "leaf", SIBLING)

    def info(lower, first):
        return jnp.stack([lower, first, core]).astype(jnp.int32).reshape(1, 3)

    def row_of(table, node):
        return lax.dynamic_index_in_dim(table, node, 0, keepdims=False).reshape(RANK, 1)

    node = ((RANK, SAMP), F32)
    mid_share, top_share = RANK // 16, RANK // 32
    mid_info = info(core, core * RANK + row * mid_share)
    stack, picked, skel, send = call(
        stack_kernel, [((2 * RANK, EXT), F32), node, ((RANK, 2 * DIM), F32), ((HALF, EXT), F32)], 1, 7,
        name="mid_stack", flops=10**9,
    )(mid_info, row_of(mid_pivots, leaf >> 1), picked, skel, proj, picked_sib, skel_sib, proj_sib)
    pick_1 = lax.ppermute(send, "leaf", COUSIN)
    pick_2 = lax.ppermute(pick_1, "leaf", SIBLING)
    mid_basis, proj, send = call(
        functools.partial(mid_kernel, mid_share),
        [((mid_share, RANK), F32), node, ((HALF, SAMP), F32)], 1, 4, SOLVE_SCRATCH,
        name="mid_solve", flops=3 * 10**9,
    )(mid_info, stack, picked, proj, proj_sib)
    proj_1 = lax.ppermute(send, "leaf", COUSIN)
    proj_2 = lax.ppermute(proj_1, "leaf", SIBLING)
    second = leaf >> 1 & 1
    (top_basis,) = call(
        functools.partial(top_kernel, top_share), [((top_share, RANK), F32)], 1, 8,
        [VMEM((2 * RANK, EXT), F32), *SOLVE_SCRATCH], name="top", flops=3 * 10**9,
    )(
        info(second, second * RANK + core * (RANK // 2) + row * top_share), row_of(top_pivots, leaf >> 2),
        picked, skel, proj, pick_1, pick_2, proj_1, proj_2,
    )
    return (leaf_basis, mid_basis, top_basis)


def solution(mesh):
    split = P(("leaf", "row"), None)
    return jax.shard_map(
        body,
        mesh=mesh,
        in_specs=(split, split, split, P("leaf", None), P("leaf", None), P(), P()),
        out_specs=(split, split, split),
        check_vma=False,
    )
```
